512 devices in a mesh: section: 8 (over z_hi, x), dp: 8 (over y, core), tensor: 8 (over z_lo).
Axes of the slice: x: 4, y: 4, z: 16 (z_hi: 2, z_lo: 8; z = z_hi * 8 + z_lo), core: 2. Of those that a mesh axis runs over, the one named last changes fastest.
Arguments:
- hidden: bfloat16 [8, 1280, 8192], P('section', 'dp', 'tensor'), may hold values from -6 to 6
- w_query: bfloat16 [8, 8192, 4096], P('section', 'dp', 'tensor'), may hold values from -0.0625 to 0.0625
- key_weight_stack: bfloat16 [8, 8192, 1024], P('section', 'tensor', 'dp'), may hold values from -0.0625 to 0.0625
- value_weight_stack: bfloat16 [8, 8192, 1024], P('section', 'tensor', 'dp'), may hold values from -0.0625 to 0.0625
- image_tokens: bfloat16 [8, 128, 8192], P('dp', 'section', 'tensor'), may hold values from -6 to 6
- score_bias: float32 [1280, 128], P('dp'), may hold values from -4 to 404, as said below
- gate_logit: float32 [8], P('section'), may hold values from 0.3 to 1.5
- cotangent: bfloat16 [8, 1280, 4096], P('section', 'dp', 'tensor'), may hold values from -48 to 48
Outputs:
- gated_output: bfloat16 [8, 1280, 4096], P('section', 'dp', 'tensor')
- image_grad: float32 [8, 128, 8192], P('dp', 'section', 'tensor')
The draws below stay inside these ranges and needn't reach their ends.
Inputs may be any that keep to these rules, and one draw needn't show every extreme that they name: `score_bias`: additive bias on the attention scores of each text token and image token.
All inputs are finite; a program needn't handle non-finite values.
Results may differ from the reference program's by a relative error of at most 0.0079.
Values may be sent and summed in bfloat16 or wider, within the bound.
No kernel may reach another device: no remote copies, remote signals or barrier semaphores. Data moves between devices by JAX's collectives and lax.ppermute only.
A program may use at most 64 MiB of HBM per device.

```python
import jax
import jax.numpy as jnp
from jax import lax

MODEL_WIDTH = 8192
QUERY_HEADS = 32
KEY_VALUE_HEADS = 8
HEAD_SIZE = 128
BATCH_TOKENS = 160
IMAGE_TOKENS = 128
TOKENS = 1280
IMAGES = 8
RELAY_SECTIONS = 8
N_DP = 8


def draw_score_bias(key, part):
    key = jax.random.fold_in(key, 11)
    values_base = jnp.clip(jax.random.normal(key, (TOKENS, IMAGE_TOKENS), jnp.float32), -4.0, 4.0)
    return values_base


def block_scale(stream_key, dims, shards, least, high):
    loudness, own = 1.0, jax.random.fold_in(stream_key, 6)
    for dim, blocks in shards:
        steps = jnp.exp(jax.random.uniform(jax.random.fold_in(own, dim), (blocks,), jnp.float32, least / len(shards), high / len(shards)))
        loudness = loudness * jnp.repeat(steps, dims[dim] // blocks).reshape([-1 if axis == dim else 1 for axis in range(len(dims))])
    return loudness


def normal_values(stream_key, dims, scale, most, shards=(), dtype=jnp.bfloat16):
    level = block_scale(stream_key, dims, shards, -0.22, 0.18) if shards else 1.0
    result = jax.random.normal(stream_key, dims, jnp.float32) * scale * level
    return jnp.minimum(jnp.maximum(result, -most), most).astype(dtype)


def setup_inputs(seed: int = 0) -> dict:
    key_list = jax.random.split(jax.random.key(seed), 9)
    return {
        "hidden": normal_values(key_list[0], (RELAY_SECTIONS, TOKENS, MODEL_WIDTH), 1.0, 6.0, ((0, 8), (1, 8), (2, 8))),
        "w_query": normal_values(key_list[1], (RELAY_SECTIONS, MODEL_WIDTH, QUERY_HEADS * HEAD_SIZE), MODEL_WIDTH ** -0.5, 0.0625, ((0, 8), (1, 8), (2, 8))),
        "key_weight_stack": normal_values(key_list[2], (RELAY_SECTIONS, MODEL_WIDTH, KEY_VALUE_HEADS * HEAD_SIZE), MODEL_WIDTH ** -0.5, 0.0625, ((0, 8), (1, 8), (2, 8))),
        "value_weight_stack": normal_values(key_list[3], (RELAY_SECTIONS, MODEL_WIDTH, KEY_VALUE_HEADS * HEAD_SIZE), MODEL_WIDTH ** -0.5, 0.0625, ((0, 8), (1, 8), (2, 8))),
        "image_tokens": normal_values(key_list[4], (IMAGES, IMAGE_TOKENS, MODEL_WIDTH), 1.0, 6.0, ((0, 8), (1, 8), (2, 8))),
        "score_bias": draw_score_bias(jax.random.fold_in(key_list[8], 71), 0),
        "gate_logit": jnp.clip(0.3 + 1.2 * jax.random.uniform(key_list[6], (RELAY_SECTIONS,), jnp.float32) ** block_scale(key_list[6], (RELAY_SECTIONS,), ((0, 8),), -0.2, 0.2), 0.3, 1.5),
        "cotangent": normal_values(key_list[7], (RELAY_SECTIONS, TOKENS, QUERY_HEADS * HEAD_SIZE), 8.0, 48.0, ((0, 8), (1, 8), (2, 8))),
    }


def rounded_values(values):
    return lax.optimization_barrier(values.astype(jnp.bfloat16)).astype(jnp.float32)


def reference(hidden, w_query, key_weight_stack, value_weight_stack, image_tokens, score_bias, gate_logit, cotangent):
    query_group_size = QUERY_HEADS // KEY_VALUE_HEADS
    scaling = HEAD_SIZE ** -0.5
    flat_images = image_tokens.reshape(N_DP * IMAGE_TOKENS, MODEL_WIDTH)
    bias_view = score_bias.reshape(N_DP, 1, 1, BATCH_TOKENS, IMAGE_TOKENS)

    def section_step(running, inputs):
        hidden_s, query_w, key_weight, value_weight, gate_s, cotangent_section = inputs
        query_input = jnp.dot(hidden_s, query_w, preferred_element_type=jnp.float32).astype(jnp.bfloat16)
        key_projected = jnp.dot(flat_images, key_weight, preferred_element_type=jnp.float32).astype(jnp.bfloat16)
        value_projected = jnp.dot(flat_images, value_weight, preferred_element_type=jnp.float32).astype(jnp.bfloat16)
        query_float = query_input.astype(jnp.float32).reshape(N_DP, BATCH_TOKENS, KEY_VALUE_HEADS, query_group_size, HEAD_SIZE)
        key_float = key_projected.astype(jnp.float32).reshape(N_DP, IMAGE_TOKENS, KEY_VALUE_HEADS, HEAD_SIZE)
        value_float = value_projected.astype(jnp.float32).reshape(N_DP, IMAGE_TOKENS, KEY_VALUE_HEADS, HEAD_SIZE)
        scores = jnp.einsum('ntkgh,nikh->nkgti', query_float, key_float) * scaling + bias_view
        row_max = jnp.max(scores, axis=-1, keepdims=True)
        exponent = jnp.exp(scores - row_max)
        attn_weights = exponent / jnp.sum(exponent, axis=-1, keepdims=True)
        weights_low = rounded_values(attn_weights)
        attended = jnp.einsum('nkgti,nikh->ntkgh', weights_low, value_float)
        scale_factor = jnp.tanh(gate_s)
        gated_out = (scale_factor * attended).astype(jnp.bfloat16).reshape(TOKENS, QUERY_HEADS * HEAD_SIZE)
        attended_gradient = rounded_values(scale_factor * cotangent_section.astype(jnp.float32)).reshape(N_DP, BATCH_TOKENS, KEY_VALUE_HEADS, query_group_size, HEAD_SIZE)
        value_gradient = jnp.einsum('nkgti,ntkgh->nikh', weights_low, attended_gradient).astype(jnp.bfloat16)
        grad_weights = jnp.einsum('ntkgh,nikh->nkgti', attended_gradient, value_float)
        grad_scores = attn_weights * (grad_weights - jnp.sum(attn_weights * grad_weights, axis=-1, keepdims=True))
        grad_low = rounded_values(grad_scores)
        key_gradient = (jnp.einsum('nkgti,ntkgh->nikh', grad_low, query_float) * scaling).astype(jnp.bfloat16)
        section_gradient = jnp.dot(key_gradient.reshape(N_DP * IMAGE_TOKENS, KEY_VALUE_HEADS * HEAD_SIZE), key_weight.T, preferred_element_type=jnp.float32)
        section_gradient = section_gradient + jnp.dot(value_gradient.reshape(N_DP * IMAGE_TOKENS, KEY_VALUE_HEADS * HEAD_SIZE), value_weight.T, preferred_element_type=jnp.float32)
        return running + section_gradient, gated_out

    initial = jnp.zeros((N_DP * IMAGE_TOKENS, MODEL_WIDTH), jnp.float32)
    summed, outputs = lax.scan(section_step, initial, (hidden, w_query, key_weight_stack, value_weight_stack, gate_logit, cotangent))
    return outputs, summed.reshape(N_DP, IMAGE_TOKENS, MODEL_WIDTH)
```

```python
import jax
import jax.numpy as jnp
from jax import lax
from jax.sharding import PartitionSpec as P

HEAD_SIZE = 128
X_SIZE = 4
Y_SIZE = 4
BF16 = jnp.bfloat16
F32 = jnp.float32


def x_shift(a, k):
    pairs = [
        (z * X_SIZE + x, z * X_SIZE + (x + k) % X_SIZE) for z in range(2) for x in range(X_SIZE)
    ]
    return lax.ppermute(a, "section", pairs)


def z_swap(a):
    return lax.ppermute(a, "section", [(s, (s + X_SIZE) % (2 * X_SIZE)) for s in range(2 * X_SIZE)])


def y_shift(a, k):
    pairs = [(y * 2 + c, ((y + k) % Y_SIZE) * 2 + c) for y in range(Y_SIZE) for c in range(2)]
    return lax.ppermute(a, "dp", pairs)


def core_swap(a):
    return lax.ppermute(a, "dp", [(d, d ^ 1) for d in range(2 * Y_SIZE)])


def gather_dp(a):
    half = a.shape[0] // 2
    before = y_shift(a, 1)
    after = y_shift(a, -1)
    opposite = jnp.concatenate([y_shift(before[:half], 1), y_shift(after[half:], -1)], axis=0)
    mine = [a, before, opposite, after]
    return [b for block in mine for b in (block, core_swap(block))]


def local(
    hidden,
    w_query,
    key_weight_stack,
    value_weight_stack,
    image_tokens,
    score_bias,
    gate_logit,
    cotangent,
):
    tok_rows = hidden.shape[1]
    columns = w_query.shape[2]
    groups = columns // HEAD_SIZE
    scaling = HEAD_SIZE ** (-0.5)
    section = lax.axis_index("section")
    dp = lax.axis_index("dp")
    z_hi, x = section // X_SIZE, section % X_SIZE
    y, core = dp // 2, dp % 2
    dp_of = [((y - k) % Y_SIZE) * 2 + (core ^ m) for k in range(Y_SIZE) for m in range(2)]
    section_of = [
        (z_hi ^ m) * X_SIZE + (x - k) % X_SIZE for k in range(X_SIZE) for m in range(2)
    ]

    features = lax.all_gather(hidden[0], "tensor", axis=0)

    own = image_tokens[0]
    both = jnp.stack([own, z_swap(own)])
    image_rows = jnp.stack([both, x_shift(both, 1), x_shift(both, 2), x_shift(both, -1)])
    image_rows = image_rows.reshape(-1, own.shape[1])
    image_count = image_rows.shape[0]

    pair_weights = gather_dp(jnp.concatenate([key_weight_stack[0], value_weight_stack[0]], axis=1))
    pair_weights = jnp.stack(pair_weights)
    portions = jnp.einsum("if,wfh->wih", image_rows, pair_weights, preferred_element_type=F32)
    portions = portions.astype(BF16)
    ordered = jnp.zeros_like(portions)
    for slot, d in enumerate(dp_of):
        ordered = lax.dynamic_update_index_in_dim(ordered, portions[slot], d, 0)
    arrived = lax.all_to_all(ordered, "tensor", 0, 0)
    own_pairs = jnp.sum(arrived.astype(F32), axis=0).astype(BF16)
    keys, values = own_pairs[:, :HEAD_SIZE], own_pairs[:, HEAD_SIZE:]

    query_weights = gather_dp(w_query[0])
    query = jnp.zeros((tok_rows, columns), F32)
    for slot, d in enumerate(dp_of):
        block = lax.dynamic_index_in_dim(features, d, 0, keepdims=False)
        query = query + jnp.dot(block, query_weights[slot], preferred_element_type=F32)
    query = query.astype(BF16).reshape(tok_rows, groups, HEAD_SIZE)

    bias = jnp.concatenate(
        [lax.dynamic_slice_in_dim(score_bias, s * own.shape[0], own.shape[0], 1) for s in section_of],
        axis=1,
    )
    scores = jnp.einsum("tgh,ih->gti", query, keys, preferred_element_type=F32) * scaling
    scores = scores + bias[None]
    row_max = jnp.max(scores, axis=-1, keepdims=True)
    exponent = jnp.exp(scores - row_max)
    attn_weights = exponent / jnp.sum(exponent, axis=-1, keepdims=True)
    weights_low = attn_weights.astype(BF16)
    attended = jnp.einsum("gti,ih->tgh", weights_low, values, preferred_element_type=F32)
    scale_factor = jnp.tanh(gate_logit[0])
    gated_out = (scale_factor * attended).astype(BF16).reshape(1, tok_rows, columns)
    attended_gradient = (scale_factor * cotangent[0].astype(F32)).astype(BF16)
    attended_gradient = attended_gradient.reshape(tok_rows, groups, HEAD_SIZE)
    value_gradient = jnp.einsum(
        "gti,tgh->ih", weights_low, attended_gradient, preferred_element_type=F32
    ).astype(BF16)
    grad_weights = jnp.einsum("tgh,ih->gti", attended_gradient, values, preferred_element_type=F32)
    grad_scores = attn_weights * (
        grad_weights - jnp.sum(attn_weights * grad_weights, axis=-1, keepdims=True)
    )
    grad_low = grad_scores.astype(BF16)
    key_gradient = jnp.einsum("gti,tgh->ih", grad_low, query, preferred_element_type=F32) * scaling
    packed = jnp.concatenate([key_gradient.astype(BF16), value_gradient], axis=1)

    copies = jnp.broadcast_to(packed[None], (2 * Y_SIZE, *packed.shape))
    every_gradient = lax.all_to_all(copies, "tensor", 0, 0)
    ordered_gradient = jnp.stack(
        [lax.dynamic_index_in_dim(every_gradient, d, 0, keepdims=False) for d in dp_of]
    )
    partial_grad = jnp.einsum(
        "wih,wfh->if", ordered_gradient, pair_weights, preferred_element_type=F32
    )
    blocks = partial_grad.reshape(X_SIZE, 2, own.shape[0], own.shape[1])
    summed = blocks[0]
    for k, shift in ((1, -1), (2, 2), (3, 1)):
        summed = summed + x_shift(blocks[k].astype(BF16), shift).astype(F32)
    image_grad = summed[0] + z_swap(summed[1])
    return (gated_out, image_grad[None])


def solution(mesh):
    in_specs = (
        P("section", "dp", "tensor"),
        P("section", "dp", "tensor"),
        P("section", "tensor", "dp"),
        P("section", "tensor", "dp"),
        P("dp", "section", "tensor"),
        P("dp", None),
        P("section"),
        P("section", "dp", "tensor"),
    )
    out_specs = (P("section", "dp", "tensor"), P("dp", "section", "tensor"))
    return jax.shard_map(local, mesh=mesh, in_specs=in_specs, out_specs=out_specs, check_vma=False)
```

```python
import functools

import jax
import jax.numpy as jnp
from jax import lax
from jax.experimental import pallas as pl
from jax.experimental.pallas import tpu as pltpu
from jax.sharding import PartitionSpec as P

HEAD_SIZE = 128
X_SIZE = 4
Y_SIZE = 4
N_BLOCKS = 8
BF16 = jnp.bfloat16
F32 = jnp.float32
VMEM = pl.BlockSpec(memory_space=pltpu.VMEM)
SMEM = pl.BlockSpec(memory_space=pltpu.SMEM)
BY_ROWS = (((0,), (0,)), ((), ()))
BY_COLUMNS = (((1,), (1,)), ((), ()))


def x_shift(a, k):
    pairs = [
        (z * X_SIZE + x, z * X_SIZE + (x + k) % X_SIZE) for z in range(2) for x in range(X_SIZE)
    ]
    return lax.ppermute(a, "section", pairs)


def z_swap(a):
    return lax.ppermute(a, "section", [(s, (s + X_SIZE) % (2 * X_SIZE)) for s in range(2 * X_SIZE)])


def y_shift(a, k):
    pairs = [(y * 2 + c, ((y + k) % Y_SIZE) * 2 + c) for y in range(Y_SIZE) for c in range(2)]
    return lax.ppermute(a, "dp", pairs)


def core_swap(a):
    return lax.ppermute(a, "dp", [(d, d ^ 1) for d in range(2 * Y_SIZE)])


def dot(a, b, dims=None):
    if dims is None:
        return jnp.dot(a, b, preferred_element_type=F32)
    return lax.dot_general(a, b, dims, preferred_element_type=F32)


def call(kernel, outs, in_specs, args, limit=32 << 20):
    return pl.pallas_call(
        kernel,
        out_shape=outs,
        in_specs=in_specs,
        out_specs=jax.tree.map(lambda _: VMEM, outs),
        compiler_params=pltpu.CompilerParams(vmem_limit_bytes=limit),
    )(*args)


def pair_kernel(dp_ref, i0, i1, i2, i3, *refs):
    weights, out = refs[:-1], refs[-1]
    rows = jnp.concatenate([r[...].reshape(-1, r.shape[-1]) for r in (i0, i1, i2, i3)], axis=0)
    for slot, w in enumerate(weights):
        out[dp_ref[slot]] = dot(rows, w[...]).astype(BF16)


def query_kernel(dp_ref, features, *refs):
    weights, out = refs[:-1], refs[-1]
    total = dot(features[dp_ref[0]], weights[0][...])
    for slot in range(1, N_BLOCKS):
        total = total + dot(features[dp_ref[slot]], weights[slot][...])
    out[...] = total.astype(BF16)


def attention_kernel(query, arrived, bias_ref, cotangent, gate, gated, packed):
    pairs = jnp.sum(arrived[...].astype(F32), axis=0).astype(BF16)
    keys, values = pairs[:, :HEAD_SIZE], pairs[:, HEAD_SIZE:]
    scaling = HEAD_SIZE ** (-0.5)
    scale_factor = jnp.tanh(gate[...])
    bias = bias_ref[...]
    key_gradient = jnp.zeros((keys.shape[0], HEAD_SIZE), F32)
    value_gradient = key_gradient
    for g in range(query.shape[1] // HEAD_SIZE):
        cols = slice(g * HEAD_SIZE, (g + 1) * HEAD_SIZE)
        q = query[:, cols]
        scores = dot(q, keys, BY_COLUMNS) * scaling + bias
        exponent = jnp.exp(scores - jnp.max(scores, axis=-1, keepdims=True))
        attn_weights = exponent / jnp.sum(exponent, axis=-1, keepdims=True)
        weights_low = attn_weights.astype(BF16)
        gated[:, cols] = (scale_factor * dot(weights_low, values)).astype(BF16)
        attended_gradient = (scale_factor * cotangent[:, cols].astype(F32)).astype(BF16)
        value_gradient += dot(weights_low, attended_gradient, BY_ROWS)
        grad_weights = dot(attended_gradient, values, BY_COLUMNS)
        inner = jnp.sum(attn_weights * grad_weights, axis=-1, keepdims=True)
        grad_low = (attn_weights * (grad_weights - inner)).astype(BF16)
        key_gradient += dot(grad_low, q, BY_ROWS)
    pair = jnp.concatenate(
        [(key_gradient * scaling).astype(BF16), value_gradient.astype(BF16)], axis=1
    )
    for t in range(N_BLOCKS):
        packed[t] = pair


def image_kernel(dp_ref, gradients, *refs):
    weights, outs = refs[:N_BLOCKS], refs[N_BLOCKS:]
    total = dot(gradients[dp_ref[0]], weights[0][...], BY_COLUMNS)
    for slot in range(1, N_BLOCKS):
        total = total + dot(gradients[dp_ref[slot]], weights[slot][...], BY_COLUMNS)
    size = total.shape[0] // X_SIZE
    for k, out in enumerate(outs):
        out[...] = total[k * size : (k + 1) * size].astype(out.dtype)


def local(
    hidden,
    w_query,
    key_weight_stack,
    value_weight_stack,
    image_tokens,
    score_bias,
    gate_logit,
    cotangent,
):
    tok_rows = hidden.shape[1]
    columns = w_query.shape[2]
    section = lax.axis_index("section")
    dp = lax.axis_index("dp")
    z_hi, x = section // X_SIZE, section % X_SIZE
    y, core = dp // 2, dp % 2
    dp_of = [((y - k) % Y_SIZE) * 2 + (core ^ m) for k in range(Y_SIZE) for m in range(2)]
    dp_order = jnp.stack(dp_of).astype(jnp.int32)
    section_of = [
        (z_hi ^ m) * X_SIZE + (x - k) % X_SIZE for k in range(X_SIZE) for m in range(2)
    ]

    features = lax.all_gather(hidden[0], "tensor", axis=0)

    own = image_tokens[0]
    both = jnp.stack([own, z_swap(own)])
    images = [both, x_shift(both, 1), x_shift(both, 2), x_shift(both, -1)]
    image_count = 8 * own.shape[0]
    width = own.shape[1]

    pair = jnp.concatenate([key_weight_stack[0], value_weight_stack[0]], axis=1)
    pair_blocks = [pair, y_shift(pair, 1), y_shift(pair, 2), y_shift(pair, -1)]
    pair_weights = [w for b in pair_blocks for w in (b, core_swap(b))]
    portions = call(
        pair_kernel,
        jax.ShapeDtypeStruct((N_BLOCKS, image_count, 2 * HEAD_SIZE), BF16),
        [SMEM] + [VMEM] * 12,
        (dp_order, *images, *pair_weights),
    )
    arrived = lax.all_to_all(portions, "tensor", 0, 0)

    w = w_query[0]
    half = w.shape[0] // 2
    before, after = y_shift(w, 1), y_shift(w, -1)
    opposite = jnp.concatenate([y_shift(before[:half], 1), y_shift(after[half:], -1)], axis=0)
    query_weights = [v for b in (w, before, opposite, after) for v in (b, core_swap(b))]
    query = call(
        query_kernel,
        jax.ShapeDtypeStruct((tok_rows, columns), BF16),
        [SMEM] + [VMEM] * 9,
        (dp_order, features, *query_weights),
    )

    bias = jnp.concatenate(
        [lax.dynamic_slice_in_dim(score_bias, s * own.shape[0], own.shape[0], 1) for s in section_of],
        axis=1,
    )
    gated_out, copies = call(
        attention_kernel,
        (
            jax.ShapeDtypeStruct((tok_rows, columns), BF16),
            jax.ShapeDtypeStruct((N_BLOCKS, image_count, 2 * HEAD_SIZE), BF16),
        ),
        [VMEM] * 5,
        (query, arrived, bias, cotangent[0], gate_logit.reshape(1, 1)),
    )

    every_gradient = lax.all_to_all(copies, "tensor", 0, 0)
    rows = image_count // X_SIZE
    mine, *away = call(
        image_kernel,
        [jax.ShapeDtypeStruct((rows, width), F32)]
        + [jax.ShapeDtypeStruct((rows, width), BF16)] * 3,
        [SMEM] + [VMEM] * 9,
        (dp_order, every_gradient, *pair_weights),
    )
    for block, shift in zip(away, (-1, 2, 1)):
        mine = mine + x_shift(block, shift).astype(F32)
    size = own.shape[0]
    image_grad = mine[:size] + z_swap(mine[size:])
    return (gated_out[None], image_grad[None])


def solution(mesh):
    in_specs = (
        P("section", "dp", "tensor"),
        P("section", "dp", "tensor"),
        P("section", "tensor", "dp"),
        P("section", "tensor", "dp"),
        P("dp", "section", "tensor"),
        P("dp", None),
        P("section"),
        P("section", "dp", "tensor"),
    )
    out_specs = (P("section", "dp", "tensor"), P("dp", "section", "tensor"))
    return jax.shard_map(local, mesh=mesh, in_specs=in_specs, out_specs=out_specs, check_vma=False)
```

```python
import jax
import jax.numpy as jnp
from jax import lax
from jax.experimental import pallas as pl
from jax.experimental.pallas import tpu as pltpu
from jax.sharding import PartitionSpec as P

HEAD_SIZE = 128
Y_SIZE = 4
N_BLOCKS = 8
BF16 = jnp.bfloat16
F32 = jnp.float32
VMEM = pl.BlockSpec(memory_space=pltpu.VMEM)
SMEM = pl.BlockSpec(memory_space=pltpu.SMEM)
BY_ROWS = (((0,), (0,)), ((), ()))
BY_COLUMNS = (((1,), (1,)), ((), ()))


def y_shift(a, k):
    pairs = [(y * 2 + c, ((y + k) % Y_SIZE) * 2 + c) for y in range(Y_SIZE) for c in range(2)]
    return lax.ppermute(a, "dp", pairs)


def core_swap(a):
    return lax.ppermute(a, "dp", [(d, d ^ 1) for d in range(2 * Y_SIZE)])


def dot(a, b, dims=None):
    if dims is None:
        return jnp.dot(a, b, preferred_element_type=F32)
    return lax.dot_general(a, b, dims, preferred_element_type=F32)


def call(kernel, outs, in_specs, args, limit=32 << 20):
    return pl.pallas_call(
        kernel,
        out_shape=outs,
        in_specs=in_specs,
        out_specs=jax.tree.map(lambda _: VMEM, outs),
        compiler_params=pltpu.CompilerParams(vmem_limit_bytes=limit),
    )(*args)


def pair_kernel(dp_ref, images, *refs):
    weights, out = refs[:-1], refs[-1]
    rows = images[...].reshape(-1, images.shape[-1])
    for slot, w in enumerate(weights):
        out[dp_ref[slot]] = dot(rows, w[...]).astype(BF16)


def query_kernel(dp_ref, features, *refs):
    weights, out = refs[:-1], refs[-1]
    total = dot(features[dp_ref[0]], weights[0][...])
    for slot in range(1, N_BLOCKS):
        total = total + dot(features[dp_ref[slot]], weights[slot][...])
    out[...] = total.astype(BF16)


def attention_kernel(query, arrived, bias_ref, cotangent, gate, gated, packed):
    pairs = jnp.sum(arrived[...].astype(F32), axis=0).astype(BF16)
    keys, values = pairs[:, :HEAD_SIZE], pairs[:, HEAD_SIZE:]
    scaling = HEAD_SIZE ** (-0.5)
    scale_factor = jnp.tanh(gate[...])
    bias = bias_ref[...]
    key_gradient = jnp.zeros((keys.shape[0], HEAD_SIZE), F32)
    value_gradient = key_gradient
    for g in range(query.shape[1] // HEAD_SIZE):
        cols = slice(g * HEAD_SIZE, (g + 1) * HEAD_SIZE)
        q = query[:, cols]
        scores = dot(q, keys, BY_COLUMNS) * scaling + bias
        exponent = jnp.exp(scores - jnp.max(scores, axis=-1, keepdims=True))
        attn_weights = exponent / jnp.sum(exponent, axis=-1, keepdims=True)
        weights_low = attn_weights.astype(BF16)
        gated[:, cols] = (scale_factor * dot(weights_low, values)).astype(BF16)
        attended_gradient = (scale_factor * cotangent[:, cols].astype(F32)).astype(BF16)
        value_gradient += dot(weights_low, attended_gradient, BY_ROWS)
        grad_weights = dot(attended_gradient, values, BY_COLUMNS)
        inner = jnp.sum(attn_weights * grad_weights, axis=-1, keepdims=True)
        grad_low = (attn_weights * (grad_weights - inner)).astype(BF16)
        key_gradient += dot(grad_low, q, BY_ROWS)
    pair = jnp.concatenate(
        [(key_gradient * scaling).astype(BF16), value_gradient.astype(BF16)], axis=1
    )
    for t in range(N_BLOCKS):
        packed[t] = pair


def image_kernel(dp_ref, gradients, *refs):
    weights, out = refs[:-1], refs[-1]
    total = dot(gradients[dp_ref[0]], weights[0][...], BY_COLUMNS)
    for slot in range(1, N_BLOCKS):
        total = total + dot(gradients[dp_ref[slot]], weights[slot][...], BY_COLUMNS)
    out[...] = total.astype(BF16)


def local(
    hidden,
    w_query,
    key_weight_stack,
    value_weight_stack,
    image_tokens,
    score_bias,
    gate_logit,
    cotangent,
):
    tok_rows = hidden.shape[1]
    columns = w_query.shape[2]
    dp = lax.axis_index("dp")
    y, core = dp >> 1, dp & 1
    dp_order = jnp.stack(
        [(((y - k) & (Y_SIZE - 1)) << 1) | (core ^ m) for k in range(Y_SIZE) for m in range(2)]
    ).astype(jnp.int32)

    features = lax.all_gather(hidden[0], "tensor", axis=0)

    own = image_tokens[0]
    images = [lax.all_to_all(jnp.broadcast_to(own[None], (8, *own.shape)), "section", 0, 0)]
    image_count = 8 * own.shape[0]
    width = own.shape[1]

    pair = jnp.concatenate([key_weight_stack[0], value_weight_stack[0]], axis=1)
    pair_blocks = [pair, y_shift(pair, 1), y_shift(pair, 2), y_shift(pair, -1)]
    pair_weights = [w for b in pair_blocks for w in (b, core_swap(b))]
    portions = call(
        pair_kernel,
        jax.ShapeDtypeStruct((N_BLOCKS, image_count, 2 * HEAD_SIZE), BF16),
        [SMEM] + [VMEM] * 9,
        (dp_order, *images, *pair_weights),
    )
    arrived = lax.all_to_all(portions, "tensor", 0, 0)

    w = w_query[0]
    half = w.shape[0] // 2
    before, after = y_shift(w, 1), y_shift(w, -1)
    opposite = jnp.concatenate([y_shift(before[:half], 1), y_shift(after[half:], -1)], axis=0)
    query_weights = [v for b in (w, before, opposite, after) for v in (b, core_swap(b))]
    query = call(
        query_kernel,
        jax.ShapeDtypeStruct((tok_rows, columns), BF16),
        [SMEM] + [VMEM] * 9,
        (dp_order, features, *query_weights),
    )

    gated_out, copies = call(
        attention_kernel,
        (
            jax.ShapeDtypeStruct((tok_rows, columns), BF16),
            jax.ShapeDtypeStruct((N_BLOCKS, image_count, 2 * HEAD_SIZE), BF16),
        ),
        [VMEM] * 5,
        (query, arrived, score_bias, cotangent[0], gate_logit.reshape(1, 1)),
    )

    every_gradient = lax.all_to_all(copies, "tensor", 0, 0)
    portion = call(
        image_kernel,
        jax.ShapeDtypeStruct((image_count, width), BF16),
        [SMEM] + [VMEM] * 9,
        (dp_order, every_gradient, *pair_weights),
    )
    portion = portion.reshape(8, *own.shape)
    image_grad = jnp.sum(lax.all_to_all(portion, "section", 0, 0).astype(F32), axis=0)
    return (gated_out[None], image_grad[None])


def solution(mesh):
    in_specs = (
        P("section", "dp", "tensor"),
        P("section", "dp", "tensor"),
        P("section", "tensor", "dp"),
        P("section", "tensor", "dp"),
        P("dp", "section", "tensor"),
        P("dp", None),
        P("section"),
        P("section", "dp", "tensor"),
    )
    out_specs = (P("section", "dp", "tensor"), P("dp", "section", "tensor"))
    return jax.shard_map(local, mesh=mesh, in_specs=in_specs, out_specs=out_specs, check_vma=False)
```

```python
import jax
import jax.numpy as jnp
from jax import lax
from jax.experimental import pallas as pl
from jax.experimental.pallas import tpu as pltpu
from jax.sharding import PartitionSpec as P

HEAD_SIZE = 128
X_SIZE = 4
Y_SIZE = 4
N_BLOCKS = 8
BF16 = jnp.bfloat16
F32 = jnp.float32
VMEM = pl.BlockSpec(memory_space=pltpu.VMEM)
SMEM = pl.BlockSpec(memory_space=pltpu.SMEM)
BY_ROWS = (((0,), (0,)), ((), ()))
BY_COLUMNS = (((1,), (1,)), ((), ()))


def z_swap(a):
    return lax.ppermute(a, "section", [(s, (s + X_SIZE) % (2 * X_SIZE)) for s in range(2 * X_SIZE)])


def x_exchange(a):
    groups = [[z * X_SIZE + x for x in range(X_SIZE)] for z in range(2)]
    return lax.all_to_all(a, "section", 0, 0, axis_index_groups=groups)


def t_swap(a, k):
    return lax.ppermute(a, "tensor", [(t, t ^ k) for t in range(8)])


def y_shift(a, k):
    pairs = [(y * 2 + c, ((y + k) % Y_SIZE) * 2 + c) for y in range(Y_SIZE) for c in range(2)]
    return lax.ppermute(a, "dp", pairs)


def core_swap(a):
    return lax.ppermute(a, "dp", [(d, d ^ 1) for d in range(2 * Y_SIZE)])


def dot(a, b, dims=None):
    if dims is None:
        return jnp.dot(a, b, preferred_element_type=F32)
    return lax.dot_general(a, b, dims, preferred_element_type=F32)


def call(kernel, outs, in_specs, args, scratch=(), limit=10 << 20):
    return pl.pallas_call(
        kernel,
        out_shape=outs,
        in_specs=in_specs,
        out_specs=jax.tree.map(lambda _: VMEM, outs),
        scratch_shapes=scratch,
        compiler_params=pltpu.CompilerParams(vmem_limit_bytes=limit),
    )(*args)


def spread_kernel(own, other, out):
    for x in range(X_SIZE):
        out[x, 0] = own[...]
        out[x, 1] = other[...]


def pair_kernel(place_ref, half_ref, images, *refs):
    weights, (keep, send, buffer) = refs[:N_BLOCKS], refs[N_BLOCKS:]
    rows = jnp.concatenate(
        [images[x, half_ref[0] ^ z] for z in range(2) for x in range(X_SIZE)], axis=0
    )
    for slot, w in enumerate(weights):
        buffer[place_ref[slot]] = dot(rows, w[...])
    half = N_BLOCKS // 2
    keep[...] = buffer[:half]
    send[...] = buffer[half:].astype(BF16)


def fold_kernel(kept, arrived, keep, send):
    half = keep.shape[0]
    keep[...] = kept[:half] + arrived[:half].astype(F32)
    send[...] = (kept[half:] + arrived[half:].astype(F32)).astype(BF16)


def fold(keep, arrived):
    half = (keep.shape[0] // 2, *keep.shape[1:])
    outs = (jax.ShapeDtypeStruct(half, F32), jax.ShapeDtypeStruct(half, BF16))
    return call(fold_kernel, outs, [VMEM] * 2, (keep, arrived))


def query_kernel(dp_ref, features, *refs):
    weights, (out, rows, columns, sems) = refs[:N_BLOCKS], refs[N_BLOCKS:]
    copies = []
    for slot in range(N_BLOCKS):
        copies.append(
            (
                pltpu.make_async_copy(features.at[dp_ref[slot]], rows.at[slot], sems.at[0, slot]),
                pltpu.make_async_copy(weights[slot], columns.at[slot], sems.at[1, slot]),
            )
        )
    for pair in copies:
        for copy in pair:
            copy.start()
    total = None
    for slot, pair in enumerate(copies):
        for copy in pair:
            copy.wait()
        part = dot(rows[slot], columns[slot])
        total = part if total is None else total + part
    out[...] = total.astype(BF16)


def attention_kernel(query, kept, arrived, bias_ref, cotangent, gate, gated, packed):
    pairs = (kept[...] + arrived[...].astype(F32)).astype(BF16)
    keys, values = pairs[:, :HEAD_SIZE], pairs[:, HEAD_SIZE:]
    scaling = HEAD_SIZE ** (-0.5)
    scale_factor = jnp.tanh(gate[...])
    bias = bias_ref[...]
    key_gradient = jnp.zeros((keys.shape[0], HEAD_SIZE), F32)
    value_gradient = key_gradient
    for g in range(query.shape[1] // HEAD_SIZE):
        cols = slice(g * HEAD_SIZE, (g + 1) * HEAD_SIZE)
        q = query[:, cols]
        scores = dot(q, keys, BY_COLUMNS) * scaling + bias
        exponent = jnp.exp(scores - jnp.max(scores, axis=-1, keepdims=True))
        attn_weights = exponent / jnp.sum(exponent, axis=-1, keepdims=True)
        weights_low = attn_weights.astype(BF16)
        gated[:, cols] = (scale_factor * dot(weights_low, values)).astype(BF16)
        attended_gradient = (scale_factor * cotangent[:, cols].astype(F32)).astype(BF16)
        value_gradient += dot(weights_low, attended_gradient, BY_ROWS)
        grad_weights = dot(attended_gradient, values, BY_COLUMNS)
        inner = jnp.sum(attn_weights * grad_weights, axis=-1, keepdims=True)
        grad_low = (attn_weights * (grad_weights - inner)).astype(BF16)
        key_gradient += dot(grad_low, q, BY_ROWS)
    packed[0] = jnp.concatenate(
        [(key_gradient * scaling).astype(BF16), value_gradient.astype(BF16)], axis=1
    )


def image_kernel(place_ref, near, far, *refs):
    weights, (out, buffer) = refs[:N_BLOCKS], refs[N_BLOCKS:]
    half = N_BLOCKS // 2
    buffer[:half] = near[...]
    buffer[half:] = far[...]
    total = dot(buffer[place_ref[0]], weights[0][...], BY_COLUMNS)
    for slot in range(1, N_BLOCKS):
        total = total + dot(buffer[place_ref[slot]], weights[slot][...], BY_COLUMNS)
    out[...] = total.astype(BF16)


def local(
    hidden,
    w_query,
    key_weight_stack,
    value_weight_stack,
    image_tokens,
    score_bias,
    gate_logit,
    cotangent,
):
    tok_rows = hidden.shape[1]
    columns = w_query.shape[2]
    dp = lax.axis_index("dp")
    slots = jnp.arange(N_BLOCKS, dtype=jnp.int32)
    dp_order = ((((dp >> 1) - (slots >> 1)) & (Y_SIZE - 1)) << 1) | ((dp ^ slots) & 1)
    apart = lax.axis_index("tensor") ^ dp_order
    place = ((apart & 1) << 2) | (apart & 2) | (apart >> 2)

    features = lax.all_gather(hidden[0], "tensor", axis=0)

    own = image_tokens[0]
    rows, width = own.shape
    pair = jnp.concatenate([key_weight_stack[0], value_weight_stack[0]], axis=1)
    cut = pair.shape[0] // 2
    first = (y_shift(pair, 1), y_shift(pair, -1), z_swap(own), core_swap(pair))
    before, behind, other, pair_swapped = lax.optimization_barrier(first)
    across = (y_shift(before[:cut], 1), y_shift(behind[cut:], -1))
    swapped = (core_swap(before), core_swap(behind))

    copies = call(
        spread_kernel,
        jax.ShapeDtypeStruct((X_SIZE, 2, rows, width), BF16),
        [VMEM] * 2,
        (own, other),
    )
    images = x_exchange(copies)
    across, swapped, images, w = lax.optimization_barrier((across, swapped, images, w_query[0]))
    opposite = jnp.concatenate(across, axis=0)
    pair_weights = [
        pair,
        pair_swapped,
        before,
        swapped[0],
        opposite,
        core_swap(opposite),
        behind,
        swapped[1],
    ]
    image_count = 2 * X_SIZE * rows
    block = (image_count, 2 * HEAD_SIZE)
    half = N_BLOCKS // 2

    keep, send = call(
        pair_kernel,
        (jax.ShapeDtypeStruct((half, *block), F32), jax.ShapeDtypeStruct((half, *block), BF16)),
        [SMEM] * 2 + [VMEM] * 9,
        (place, lax.axis_index("section")[None] >> 2, images, *pair_weights),
        [pltpu.VMEM((N_BLOCKS, *block), F32)],
    )
    before, behind = y_shift(w, 1), y_shift(w, -1)
    keep, send = fold(keep, t_swap(send, 1))
    (keep, send), before, behind = lax.optimization_barrier(((keep, send), before, behind))
    cut = w.shape[0] // 2
    across = (y_shift(before[:cut], 1), y_shift(behind[cut:], -1))
    keep, send = fold(keep, t_swap(send, 2))
    (keep, send), across, w = lax.optimization_barrier(((keep, send), across, w))
    arrived = t_swap(send, 4)
    opposite = jnp.concatenate(across, axis=0)
    query_weights = [v for b in (w, before, opposite, behind) for v in (b, core_swap(b))]
    tokens, columns = hidden.shape[1], w_query.shape[2]
    query = call(
        query_kernel,
        jax.ShapeDtypeStruct((tokens, columns), BF16),
        [SMEM] + [pl.BlockSpec(memory_space=pl.ANY)] * 9,
        (dp_order, features, *query_weights),
        [
            pltpu.VMEM(features.shape, BF16),
            pltpu.VMEM((N_BLOCKS, *w.shape), BF16),
            pltpu.SemaphoreType.DMA((2, N_BLOCKS)),
        ],
        limit=60 << 20,
    )

    gated_out, packed = call(
        attention_kernel,
        (jax.ShapeDtypeStruct((tokens, columns), BF16), jax.ShapeDtypeStruct((1, *block), BF16)),
        [VMEM] * 6,
        (query, keep[0], arrived[0], score_bias, cotangent[0], gate_logit.reshape(1, 1)),
    )

    near = jnp.concatenate([packed, t_swap(packed, 4)])
    near = jnp.concatenate([near, t_swap(near, 2)])
    far = t_swap(near, 1)
    portion = call(
        image_kernel,
        jax.ShapeDtypeStruct((image_count, width), BF16),
        [SMEM] + [VMEM] * 10,
        (place, near, far, *pair_weights),
        [pltpu.VMEM((N_BLOCKS, *block), BF16)],
    )
    portion = portion.reshape(2 * X_SIZE, rows, width)
    image_grad = jnp.sum(lax.all_to_all(portion, "section", 0, 0).astype(F32), axis=0)
    return (gated_out[None], image_grad[None])


def solution(mesh):
    in_specs = (
        P("section", "dp", "tensor"),
        P("section", "dp", "tensor"),
        P("section", "tensor", "dp"),
        P("section", "tensor", "dp"),
        P("dp", "section", "tensor"),
        P("dp", None),
        P("section"),
        P("section", "dp", "tensor"),
    )
    out_specs = (P("section", "dp", "tensor"), P("dp", "section", "tensor"))
    return jax.shard_map(local, mesh=mesh, in_specs=in_specs, out_specs=out_specs, check_vma=False)
```

```python
import jax
import jax.numpy as jnp
from jax import lax
from jax.experimental import pallas as pl
from jax.experimental.pallas import tpu as pltpu
from jax.sharding import PartitionSpec as P

HEAD_SIZE = 128
X_SIZE = 4
Y_SIZE = 4
N_BLOCKS = 8
DEPTH = 3
BF16 = jnp.bfloat16
F32 = jnp.float32
VMEM = pl.BlockSpec(memory_space=pltpu.VMEM)
SMEM = pl.BlockSpec(memory_space=pltpu.SMEM)
BY_ROWS = (((0,), (0,)), ((), ()))
BY_COLUMNS = (((1,), (1,)), ((), ()))


def z_swap(a):
    return lax.ppermute(a, "section", [(s, (s + X_SIZE) % (2 * X_SIZE)) for s in range(2 * X_SIZE)])


def x_exchange(a):
    groups = [[z * X_SIZE + x for x in range(X_SIZE)] for z in range(2)]
    return lax.all_to_all(a, "section", 0, 0, axis_index_groups=groups)


def t_swap(a, k):
    return lax.ppermute(a, "tensor", [(t, t ^ k) for t in range(8)])


def y_shift(a, k):
    pairs = [(y * 2 + c, ((y + k) % Y_SIZE) * 2 + c) for y in range(Y_SIZE) for c in range(2)]
    return lax.ppermute(a, "dp", pairs)


def y_gather(a):
    groups = [[2 * y + c for y in range(Y_SIZE)] for c in range(2)]
    copies = jnp.broadcast_to(a[None], (Y_SIZE, *a.shape))
    return lax.all_to_all(copies, "dp", 0, 0, axis_index_groups=groups)


def core_swap(a):
    return lax.ppermute(a, "dp", [(d, d ^ 1) for d in range(2 * Y_SIZE)])


def dot(a, b, dims=None):
    if dims is None:
        return jnp.dot(a, b, preferred_element_type=F32)
    return lax.dot_general(a, b, dims, preferred_element_type=F32)


def call(kernel, outs, in_specs, args, scratch=(), limit=10 << 20):
    return pl.pallas_call(
        kernel,
        out_shape=outs,
        in_specs=in_specs,
        out_specs=jax.tree.map(lambda _: VMEM, outs),
        scratch_shapes=scratch,
        compiler_params=pltpu.CompilerParams(vmem_limit_bytes=limit),
    )(*args)


def spread_kernel(own, other, out):
    for x in range(X_SIZE):
        out[x, 0] = own[...]
        out[x, 1] = other[...]


def pair_kernel(place_ref, half_ref, images, near, far, keep, send, buffer):
    rows = jnp.concatenate(
        [images[x, half_ref[0] ^ z] for z in range(2) for x in range(X_SIZE)], axis=0
    )
    for slot in range(N_BLOCKS):
        weights = (near, far)[slot % 2][slot // 2]
        buffer[place_ref[slot]] = dot(rows, weights)
    half = N_BLOCKS // 2
    keep[...] = buffer[:half]
    send[...] = buffer[half:].astype(BF16)


def fold_kernel(kept, arrived, keep, send):
    half = keep.shape[0]
    keep[...] = kept[:half] + arrived[:half].astype(F32)
    send[...] = (kept[half:] + arrived[half:].astype(F32)).astype(BF16)


def fold(keep, arrived):
    half = (keep.shape[0] // 2, *keep.shape[1:])
    outs = (jax.ShapeDtypeStruct(half, F32), jax.ShapeDtypeStruct(half, BF16))
    return call(fold_kernel, outs, [VMEM] * 2, (keep, arrived))


def attention_kernel(dp_ref, features, *refs):
    blocks, refs = refs[: 2 * N_BLOCKS - 6], refs[2 * N_BLOCKS - 6 :]
    kept, arrived, bias_ref, cotangent, gate, gated, packed, rows, columns, sems = refs
    cut = columns.shape[1] // 2
    copies = []
    for slot in range(N_BLOCKS):
        group = [pltpu.make_async_copy(features.at[dp_ref[slot]], rows.at[slot], sems.at[0, slot])]
        if slot // 2 == 2:
            for part in range(2):
                group.append(
                    pltpu.make_async_copy(
                        blocks[4 + 2 * part + slot % 2],
                        columns.at[slot, pl.ds(part * cut, cut)],
                        sems.at[1 + part, slot],
                    )
                )
        else:
            at = slot if slot < 4 else slot + 2
            group.append(pltpu.make_async_copy(blocks[at], columns.at[slot], sems.at[1, slot]))
        copies.append(group)
    for group in copies[:DEPTH]:
        for copy in group:
            copy.start()
    query = None
    for slot, group in enumerate(copies):
        for copy in group:
            copy.wait()
        if slot + DEPTH < N_BLOCKS:
            for copy in copies[slot + DEPTH]:
                copy.start()
        part = dot(rows[slot], columns[slot])
        query = part if query is None else query + part
    query = query.astype(BF16)

    pairs = (kept[...] + arrived[...].astype(F32)).astype(BF16)
    keys, values = pairs[:, :HEAD_SIZE], pairs[:, HEAD_SIZE:]
    scaling = HEAD_SIZE ** (-0.5)
    scale_factor = jnp.tanh(gate[...])
    bias = bias_ref[...]
    key_gradient = jnp.zeros((keys.shape[0], HEAD_SIZE), F32)
    value_gradient = key_gradient
    for g in range(query.shape[1] // HEAD_SIZE):
        cols = slice(g * HEAD_SIZE, (g + 1) * HEAD_SIZE)
        q = query[:, cols]
        scores = dot(q, keys, BY_COLUMNS) * scaling + bias
        exponent = jnp.exp(scores - jnp.max(scores, axis=-1, keepdims=True))
        attn_weights = exponent / jnp.sum(exponent, axis=-1, keepdims=True)
        weights_low = attn_weights.astype(BF16)
        gated[:, cols] = (scale_factor * dot(weights_low, values)).astype(BF16)
        attended_gradient = (scale_factor * cotangent[:, cols].astype(F32)).astype(BF16)
        value_gradient += dot(weights_low, attended_gradient, BY_ROWS)
        grad_weights = dot(attended_gradient, values, BY_COLUMNS)
        inner = jnp.sum(attn_weights * grad_weights, axis=-1, keepdims=True)
        grad_low = (attn_weights * (grad_weights - inner)).astype(BF16)
        key_gradient += dot(grad_low, q, BY_ROWS)
    packed[0] = jnp.concatenate(
        [(key_gradient * scaling).astype(BF16), value_gradient.astype(BF16)], axis=1
    )


def image_kernel(place_ref, own, by4, by2, by1, near, far, out, buffer):
    for at, part in ((0, own), (1, by4), (2, by2), (4, by1)):
        buffer[at : at + part.shape[0]] = part[...]
    total = None
    for slot in range(N_BLOCKS):
        weights = (near, far)[slot % 2][slot // 2]
        part = dot(buffer[place_ref[slot]], weights, BY_COLUMNS)
        total = part if total is None else total + part
    out[...] = total.astype(BF16)


def local(
    hidden,
    w_query,
    key_weight_stack,
    value_weight_stack,
    image_tokens,
    score_bias,
    gate_logit,
    cotangent,
):
    tok_rows = hidden.shape[1]
    columns = w_query.shape[2]
    dp = lax.axis_index("dp")
    slots = jnp.arange(N_BLOCKS, dtype=jnp.int32)
    dp_order = ((((dp >> 1) - (slots >> 1)) & (Y_SIZE - 1)) << 1) | ((dp ^ slots) & 1)
    apart = lax.axis_index("tensor") ^ (slots ^ (dp & 1))
    place = ((apart & 1) << 2) | (apart & 2) | (apart >> 2)

    features = lax.all_gather(hidden[0], "tensor", axis=0)

    own = image_tokens[0]
    rows, width = own.shape
    pair = jnp.concatenate([key_weight_stack[0], value_weight_stack[0]], axis=1)
    copies = call(
        spread_kernel,
        jax.ShapeDtypeStruct((X_SIZE, 2, rows, width), BF16),
        [VMEM] * 2,
        (own, z_swap(own)),
    )
    near_pairs, images = lax.optimization_barrier((y_gather(pair), x_exchange(copies)))
    far_pairs = core_swap(near_pairs)
    image_count = 2 * X_SIZE * rows
    block = (image_count, 2 * HEAD_SIZE)
    half = N_BLOCKS // 2

    keep, send = call(
        pair_kernel,
        (jax.ShapeDtypeStruct((half, *block), F32), jax.ShapeDtypeStruct((half, *block), BF16)),
        [SMEM] * 2 + [VMEM] * 3,
        (place, lax.axis_index("section")[None] >> 2, images, near_pairs, far_pairs),
        [pltpu.VMEM((N_BLOCKS, *block), F32)],
    )

    w, _ = lax.optimization_barrier((w_query[0], near_pairs))
    cut = w.shape[0] // 2
    before, behind = y_shift(w, 1), y_shift(w, -1)
    keep, send = fold(keep, t_swap(send, 1))
    (keep, send), before, behind = lax.optimization_barrier(((keep, send), before, behind))
    across = (y_shift(before[:cut], 1), y_shift(behind[cut:], -1))
    keep, send = fold(keep, t_swap(send, 2))
    (keep, send), across, w = lax.optimization_barrier(((keep, send), across, w))
    arrived = t_swap(send, 4)
    query_weights = [v for b in (w, before, *across, behind) for v in (b, core_swap(b))]

    tokens, columns = hidden.shape[1], w_query.shape[2]
    gated_out, packed = call(
        attention_kernel,
        (jax.ShapeDtypeStruct((tokens, columns), BF16), jax.ShapeDtypeStruct((1, *block), BF16)),
        [SMEM] + [pl.BlockSpec(memory_space=pl.ANY)] * 11 + [VMEM] * 5,
        (
            dp_order,
            features,
            *query_weights,
            keep[0],
            arrived[0],
            score_bias,
            cotangent[0],
            gate_logit.reshape(1, 1),
        ),
        [
            pltpu.VMEM(features.shape, BF16),
            pltpu.VMEM((N_BLOCKS, *w.shape), BF16),
            pltpu.SemaphoreType.DMA((3, N_BLOCKS)),
        ],
        limit=60 << 20,
    )

    by4 = t_swap(packed, 4)
    by2 = t_swap(jnp.concatenate([packed, by4]), 2)
    by1 = t_swap(jnp.concatenate([packed, by4, by2]), 1)
    portion = call(
        image_kernel,
        jax.ShapeDtypeStruct((image_count, width), BF16),
        [SMEM] + [VMEM] * 6,
        (place, packed, by4, by2, by1, near_pairs, far_pairs),
        [pltpu.VMEM((N_BLOCKS, *block), BF16)],
    )
    portion = portion.reshape(2 * X_SIZE, rows, width)
    image_grad = jnp.sum(lax.all_to_all(portion, "section", 0, 0).astype(F32), axis=0)
    return (gated_out[None], image_grad[None])


def solution(mesh):
    in_specs = (
        P("section", "dp", "tensor"),
        P("section", "dp", "tensor"),
        P("section", "tensor", "dp"),
        P("section", "tensor", "dp"),
        P("dp", "section", "tensor"),
        P("dp", None),
        P("section"),
        P("section", "dp", "tensor"),
    )
    out_specs = (P("section", "dp", "tensor"), P("dp", "section", "tensor"))
    return jax.shard_map(local, mesh=mesh, in_specs=in_specs, out_specs=out_specs, check_vma=False)
```

```python
import jax
import jax.numpy as jnp
from jax import lax
from jax.experimental import pallas as pl
from jax.experimental.pallas import tpu as pltpu
from jax.sharding import PartitionSpec as P

HEAD_SIZE = 128
X_SIZE = 4
Y_SIZE = 4
N_BLOCKS = 8
DEPTH = 3
BF16 = jnp.bfloat16
F32 = jnp.float32
VMEM = pl.BlockSpec(memory_space=pltpu.VMEM)
SMEM = pl.BlockSpec(memory_space=pltpu.SMEM)
BY_ROWS = (((0,), (0,)), ((), ()))
BY_COLUMNS = (((1,), (1,)), ((), ()))


def z_swap(a):
    return lax.ppermute(a, "section", [(s, (s + X_SIZE) % (2 * X_SIZE)) for s in range(2 * X_SIZE)])


def x_exchange(a):
    groups = [[z * X_SIZE + x for x in range(X_SIZE)] for z in range(2)]
    return lax.all_to_all(a, "section", 0, 0, axis_index_groups=groups)


def t_swap(a, k):
    return lax.ppermute(a, "tensor", [(t, t ^ k) for t in range(8)])


def y_shift(a, k):
    pairs = [(y * 2 + c, ((y + k) % Y_SIZE) * 2 + c) for y in range(Y_SIZE) for c in range(2)]
    return lax.ppermute(a, "dp", pairs)


def y_gather(a):
    groups = [[2 * y + c for y in range(Y_SIZE)] for c in range(2)]
    copies = jnp.broadcast_to(a[None], (Y_SIZE, *a.shape))
    return lax.all_to_all(copies, "dp", 0, 0, axis_index_groups=groups)


def core_swap(a):
    return lax.ppermute(a, "dp", [(d, d ^ 1) for d in range(2 * Y_SIZE)])


def dot(a, b, dims=None):
    if dims is None:
        return jnp.dot(a, b, preferred_element_type=F32)
    return lax.dot_general(a, b, dims, preferred_element_type=F32)


def call(kernel, outs, in_specs, args, scratch=(), limit=10 << 20):
    return pl.pallas_call(
        kernel,
        out_shape=outs,
        in_specs=in_specs,
        out_specs=jax.tree.map(lambda _: VMEM, outs),
        scratch_shapes=scratch,
        compiler_params=pltpu.CompilerParams(vmem_limit_bytes=limit),
    )(*args)


def spread_kernel(own, other, out):
    for x in range(X_SIZE):
        out[x, 0] = own[...]
        out[x, 1] = other[...]


def pair_kernel(head_ref, half_ref, images, near, far, out):
    rows = jnp.concatenate(
        [images[x, half_ref[0] ^ z] for z in range(2) for x in range(X_SIZE)], axis=0
    )
    for slot in range(N_BLOCKS):
        weights = (near, far)[slot % 2][slot // 2]
        out[head_ref[slot]] = dot(rows, weights).astype(BF16)


def attention_kernel(dp_ref, features, *refs):
    blocks, refs = refs[: 2 * N_BLOCKS - 6], refs[2 * N_BLOCKS - 6 :]
    arrived, bias_ref, cotangent, gate, gated, packed, rows, columns, sems = refs
    cut = columns.shape[1] // 2
    copies = []
    for slot in range(N_BLOCKS):
        group = [pltpu.make_async_copy(features.at[dp_ref[slot]], rows.at[slot], sems.at[0, slot])]
        if slot // 2 == 2:
            for part in range(2):
                group.append(
                    pltpu.make_async_copy(
                        blocks[4 + 2 * part + slot % 2],
                        columns.at[slot, pl.ds(part * cut, cut)],
                        sems.at[1 + part, slot],
                    )
                )
        else:
            at = slot if slot < 4 else slot + 2
            group.append(pltpu.make_async_copy(blocks[at], columns.at[slot], sems.at[1, slot]))
        copies.append(group)
    for group in copies[:DEPTH]:
        for copy in group:
            copy.start()
    query = None
    for slot, group in enumerate(copies):
        for copy in group:
            copy.wait()
        if slot + DEPTH < N_BLOCKS:
            for copy in copies[slot + DEPTH]:
                copy.start()
        part = dot(rows[slot], columns[slot])
        query = part if query is None else query + part
    query = query.astype(BF16)

    pairs = jnp.sum(arrived[...].astype(F32), axis=0).astype(BF16)
    keys, values = pairs[:, :HEAD_SIZE], pairs[:, HEAD_SIZE:]
    scaling = HEAD_SIZE ** (-0.5)
    scale_factor = jnp.tanh(gate[...])
    bias = bias_ref[...]
    key_gradient = jnp.zeros((keys.shape[0], HEAD_SIZE), F32)
    value_gradient = key_gradient
    for g in range(query.shape[1] // HEAD_SIZE):
        cols = slice(g * HEAD_SIZE, (g + 1) * HEAD_SIZE)
        q = query[:, cols]
        scores = dot(q, keys, BY_COLUMNS) * scaling + bias
        exponent = jnp.exp(scores - jnp.max(scores, axis=-1, keepdims=True))
        attn_weights = exponent / jnp.sum(exponent, axis=-1, keepdims=True)
        weights_low = attn_weights.astype(BF16)
        gated[:, cols] = (scale_factor * dot(weights_low, values)).astype(BF16)
        attended_gradient = (scale_factor * cotangent[:, cols].astype(F32)).astype(BF16)
        value_gradient += dot(weights_low, attended_gradient, BY_ROWS)
        grad_weights = dot(attended_gradient, values, BY_COLUMNS)
        inner = jnp.sum(attn_weights * grad_weights, axis=-1, keepdims=True)
        grad_low = (attn_weights * (grad_weights - inner)).astype(BF16)
        key_gradient += dot(grad_low, q, BY_ROWS)
    packed[0] = jnp.concatenate(
        [(key_gradient * scaling).astype(BF16), value_gradient.astype(BF16)], axis=1
    )


def image_kernel(place_ref, own, by4, by2, by1, near, far, out, buffer):
    for at, part in ((0, own), (1, by4), (2, by2), (4, by1)):
        buffer[at : at + part.shape[0]] = part[...]
    total = None
    for slot in range(N_BLOCKS):
        weights = (near, far)[slot % 2][slot // 2]
        part = dot(buffer[place_ref[slot]], weights, BY_COLUMNS)
        total = part if total is None else total + part
    out[...] = total.astype(BF16)


def local(
    hidden,
    w_query,
    key_weight_stack,
    value_weight_stack,
    image_tokens,
    score_bias,
    gate_logit,
    cotangent,
):
    tok_rows = hidden.shape[1]
    columns = w_query.shape[2]
    dp = lax.axis_index("dp")
    slots = jnp.arange(N_BLOCKS, dtype=jnp.int32)
    dp_order = ((((dp >> 1) - (slots >> 1)) & (Y_SIZE - 1)) << 1) | ((dp ^ slots) & 1)
    head_order = slots ^ (dp & 1)
    apart = lax.axis_index("tensor") ^ head_order
    place = ((apart & 1) << 2) | (apart & 2) | (apart >> 2)

    features = lax.all_gather(hidden[0], "tensor", axis=0)

    own = image_tokens[0]
    rows, width = own.shape
    pair = jnp.concatenate([key_weight_stack[0], value_weight_stack[0]], axis=1)
    near_pairs, other = lax.optimization_barrier((y_gather(pair), z_swap(own)))

    copies = call(
        spread_kernel,
        jax.ShapeDtypeStruct((X_SIZE, 2, rows, width), BF16),
        [VMEM] * 2,
        (own, other),
    )
    images = x_exchange(copies)
    far_pairs = core_swap(near_pairs)
    image_count = 2 * X_SIZE * rows
    block = (image_count, 2 * HEAD_SIZE)
    portions = call(
        pair_kernel,
        jax.ShapeDtypeStruct((N_BLOCKS, *block), BF16),
        [SMEM] * 2 + [VMEM] * 3,
        (head_order, lax.axis_index("section")[None] >> 2, images, near_pairs, far_pairs),
    )
    arrived = lax.all_to_all(portions, "tensor", 0, 0)

    w, _ = lax.optimization_barrier((w_query[0], near_pairs))
    cut = w.shape[0] // 2
    before, behind = y_shift(w, 1), y_shift(w, -1)
    across = (y_shift(before[:cut], 1), y_shift(behind[cut:], -1))
    query_weights = [v for b in (w, before, *across, behind) for v in (b, core_swap(b))]

    tokens, columns = hidden.shape[1], w_query.shape[2]
    gated_out, packed = call(
        attention_kernel,
        (jax.ShapeDtypeStruct((tokens, columns), BF16), jax.ShapeDtypeStruct((1, *block), BF16)),
        [SMEM] + [pl.BlockSpec(memory_space=pl.ANY)] * 11 + [VMEM] * 4,
        (
            dp_order,
            features,
            *query_weights,
            arrived,
            score_bias,
            cotangent[0],
            gate_logit.reshape(1, 1),
        ),
        [
            pltpu.VMEM(features.shape, BF16),
            pltpu.VMEM((N_BLOCKS, *w.shape), BF16),
            pltpu.SemaphoreType.DMA((3, N_BLOCKS)),
        ],
        limit=60 << 20,
    )

    by4 = t_swap(packed, 4)
    by2 = t_swap(jnp.concatenate([packed, by4]), 2)
    by1 = t_swap(jnp.concatenate([packed, by4, by2]), 1)
    portion = call(
        image_kernel,
        jax.ShapeDtypeStruct((image_count, width), BF16),
        [SMEM] + [VMEM] * 6,
        (place, packed, by4, by2, by1, near_pairs, far_pairs),
        [pltpu.VMEM((N_BLOCKS, *block), BF16)],
    )
    portion = portion.reshape(2 * X_SIZE, rows, width)
    image_grad = jnp.sum(lax.all_to_all(portion, "section", 0, 0).astype(F32), axis=0)
    return (gated_out[None], image_grad[None])


def solution(mesh):
    in_specs = (
        P("section", "dp", "tensor"),
        P("section", "dp", "tensor"),
        P("section", "tensor", "dp"),
        P("section", "tensor", "dp"),
        P("dp", "section", "tensor"),
        P("dp", None),
        P("section"),
        P("section", "dp", "tensor"),
    )
    out_specs = (P("section", "dp", "tensor"), P("dp", "section", "tensor"))
    return jax.shard_map(local, mesh=mesh, in_specs=in_specs, out_specs=out_specs, check_vma=False)
```

```python
import jax
import jax.numpy as jnp
from jax import lax
from jax.experimental import pallas as pl
from jax.experimental.pallas import tpu as pltpu
from jax.sharding import PartitionSpec as P

HEAD_SIZE = 128
X_SIZE = 4
Y_SIZE = 4
N_BLOCKS = 8
DEPTH = 3
BF16 = jnp.bfloat16
F32 = jnp.float32
VMEM = pl.BlockSpec(memory_space=pltpu.VMEM)
SMEM = pl.BlockSpec(memory_space=pltpu.SMEM)
BY_ROWS = (((0,), (0,)), ((), ()))
BY_COLUMNS = (((1,), (1,)), ((), ()))


def z_swap(a):
    return lax.ppermute(a, "section", [(s, (s + X_SIZE) % (2 * X_SIZE)) for s in range(2 * X_SIZE)])


def x_exchange(a):
    groups = [[z * X_SIZE + x for x in range(X_SIZE)] for z in range(2)]
    return lax.all_to_all(a, "section", 0, 0, axis_index_groups=groups)


def t_swap(a, k):
    return lax.ppermute(a, "tensor", [(t, t ^ k) for t in range(8)])


def y_shift(a, k):
    pairs = [(y * 2 + c, ((y + k) % Y_SIZE) * 2 + c) for y in range(Y_SIZE) for c in range(2)]
    return lax.ppermute(a, "dp", pairs)


def y_gather(a):
    groups = [[2 * y + c for y in range(Y_SIZE)] for c in range(2)]
    copies = jnp.broadcast_to(a[None], (Y_SIZE, *a.shape))
    return lax.all_to_all(copies, "dp", 0, 0, axis_index_groups=groups)


def core_swap(a):
    return lax.ppermute(a, "dp", [(d, d ^ 1) for d in range(2 * Y_SIZE)])


def dot(a, b, dims=None):
    if dims is None:
        return jnp.dot(a, b, preferred_element_type=F32)
    return lax.dot_general(a, b, dims, preferred_element_type=F32)


def call(kernel, outs, in_specs, args, scratch=(), limit=10 << 20, cost=None):
    return pl.pallas_call(
        kernel,
        out_shape=outs,
        in_specs=in_specs,
        out_specs=jax.tree.map(lambda _: VMEM, outs),
        scratch_shapes=scratch,
        cost_estimate=cost,
        compiler_params=pltpu.CompilerParams(vmem_limit_bytes=limit),
    )(*args)


def spread_kernel(own, other, out):
    for x in range(X_SIZE):
        out[x, 0] = own[...]
        out[x, 1] = other[...]


def pair_kernel(head_ref, half_ref, images, near, far, out):
    rows = jnp.concatenate(
        [images[x, half_ref[0] ^ z] for z in range(2) for x in range(X_SIZE)], axis=0
    )
    for slot in range(N_BLOCKS):
        weights = (near, far)[slot % 2][slot // 2]
        out[head_ref[slot]] = dot(rows, weights).astype(BF16)


def query_kernel(dp_ref, features, *refs):
    blocks, (out, rows, columns, sems) = refs[:10], refs[10:]
    cut = columns.shape[1] // 2
    copies = []
    for slot in range(N_BLOCKS):
        group = [pltpu.make_async_copy(features.at[dp_ref[slot]], rows.at[slot], sems.at[0, slot])]
        if slot // 2 == 2:
            for part in range(2):
                group.append(
                    pltpu.make_async_copy(
                        blocks[4 + 2 * part + slot % 2],
                        columns.at[slot, pl.ds(part * cut, cut)],
                        sems.at[1 + part, slot],
                    )
                )
        else:
            at = slot if slot < 4 else slot + 2
            group.append(pltpu.make_async_copy(blocks[at], columns.at[slot], sems.at[1, slot]))
        copies.append(group)
    for group in copies[:DEPTH]:
        for copy in group:
            copy.start()
    total = None
    for slot, group in enumerate(copies):
        for copy in group:
            copy.wait()
        if slot + DEPTH < N_BLOCKS:
            for copy in copies[slot + DEPTH]:
                copy.start()
        part = dot(rows[slot], columns[slot])
        total = part if total is None else total + part
    out[...] = total.astype(BF16)


def attention_kernel(query, arrived, bias_ref, cotangent, gate, gated, packed):
    pairs = jnp.sum(arrived[...].astype(F32), axis=0).astype(BF16)
    keys, values = pairs[:, :HEAD_SIZE], pairs[:, HEAD_SIZE:]
    scaling = HEAD_SIZE ** (-0.5)
    scale_factor = jnp.tanh(gate[...])
    bias = bias_ref[...]
    key_gradient = jnp.zeros((keys.shape[0], HEAD_SIZE), F32)
    value_gradient = key_gradient
    for g in range(query.shape[1] // HEAD_SIZE):
        cols = slice(g * HEAD_SIZE, (g + 1) * HEAD_SIZE)
        q = query[:, cols]
        scores = dot(q, keys, BY_COLUMNS) * scaling + bias
        exponent = jnp.exp(scores - jnp.max(scores, axis=-1, keepdims=True))
        attn_weights = exponent / jnp.sum(exponent, axis=-1, keepdims=True)
        weights_low = attn_weights.astype(BF16)
        gated[:, cols] = (scale_factor * dot(weights_low, values)).astype(BF16)
        attended_gradient = (scale_factor * cotangent[:, cols].astype(F32)).astype(BF16)
        value_gradient += dot(weights_low, attended_gradient, BY_ROWS)
        grad_weights = dot(attended_gradient, values, BY_COLUMNS)
        inner = jnp.sum(attn_weights * grad_weights, axis=-1, keepdims=True)
        grad_low = (attn_weights * (grad_weights - inner)).astype(BF16)
        key_gradient += dot(grad_low, q, BY_ROWS)
    packed[0] = jnp.concatenate(
        [(key_gradient * scaling).astype(BF16), value_gradient.astype(BF16)], axis=1
    )


def image_kernel(place_ref, own, by4, by2, by1, by5, by3, near, far, out, buffer):
    for at, part in ((0, own), (1, by4), (2, by2), (4, by1), (5, by5), (6, by3)):
        buffer[at : at + part.shape[0]] = part[...]
    total = None
    for slot in range(N_BLOCKS):
        weights = (near, far)[slot % 2][slot // 2]
        part = dot(buffer[place_ref[slot]], weights, BY_COLUMNS)
        total = part if total is None else total + part
    out[...] = total.astype(BF16)


def local(
    hidden,
    w_query,
    key_weight_stack,
    value_weight_stack,
    image_tokens,
    score_bias,
    gate_logit,
    cotangent,
):
    tok_rows = hidden.shape[1]
    columns = w_query.shape[2]
    dp = lax.axis_index("dp")
    slots = jnp.arange(N_BLOCKS, dtype=jnp.int32)
    dp_order = ((((dp >> 1) - (slots >> 1)) & (Y_SIZE - 1)) << 1) | ((dp ^ slots) & 1)
    head_order = slots ^ (dp & 1)
    apart = lax.axis_index("tensor") ^ head_order
    place = ((apart & 1) << 2) | (apart & 2) | (apart >> 2)

    features = lax.all_gather(hidden[0], "tensor", axis=0)

    own = image_tokens[0]
    rows, width = own.shape
    pair = jnp.concatenate([key_weight_stack[0], value_weight_stack[0]], axis=1)
    near_pairs, other = lax.optimization_barrier((y_gather(pair), z_swap(own)))

    copies = call(
        spread_kernel,
        jax.ShapeDtypeStruct((X_SIZE, 2, rows, width), BF16),
        [VMEM] * 2,
        (own, other),
    )
    images = x_exchange(copies)
    far_pairs = core_swap(near_pairs)
    image_count = 2 * X_SIZE * rows
    block = (image_count, 2 * HEAD_SIZE)
    portions = call(
        pair_kernel,
        jax.ShapeDtypeStruct((N_BLOCKS, *block), BF16),
        [SMEM] * 2 + [VMEM] * 3,
        (head_order, lax.axis_index("section")[None] >> 2, images, near_pairs, far_pairs),
    )
    arrived = lax.all_to_all(portions, "tensor", 0, 0)

    w, _ = lax.optimization_barrier((w_query[0], near_pairs))
    cut = w.shape[0] // 2
    before, behind = y_shift(w, 1), y_shift(w, -1)
    across = (y_shift(before[:cut], 1), y_shift(behind[cut:], -1))
    query_weights = [v for b in (w, before, *across, behind) for v in (b, core_swap(b))]

    tokens, columns = hidden.shape[1], w_query.shape[2]
    query = call(
        query_kernel,
        jax.ShapeDtypeStruct((tokens, columns), BF16),
        [SMEM] + [pl.BlockSpec(memory_space=pl.ANY)] * 11,
        (dp_order, features, *query_weights),
        [
            pltpu.VMEM(features.shape, BF16),
            pltpu.VMEM((N_BLOCKS, *w.shape), BF16),
            pltpu.SemaphoreType.DMA((3, N_BLOCKS)),
        ],
        limit=60 << 20,
        cost=pl.CostEstimate(
            flops=2 * tokens * columns * N_BLOCKS * w.shape[0],
            bytes_accessed=2 * N_BLOCKS * (w.size + hidden.size),
            transcendentals=0,
        ),
    )
    gated_out, packed = call(
        attention_kernel,
        (jax.ShapeDtypeStruct((tokens, columns), BF16), jax.ShapeDtypeStruct((1, *block), BF16)),
        [VMEM] * 5,
        (query, arrived, score_bias, cotangent[0], gate_logit.reshape(1, 1)),
    )

    by4, by1 = lax.optimization_barrier((t_swap(packed, 4), t_swap(packed, 1)))
    both = jnp.concatenate([packed, by4])
    by2, by5 = lax.optimization_barrier((t_swap(both, 2), t_swap(by4, 1)))
    by3 = t_swap(by2, 1)
    portion = call(
        image_kernel,
        jax.ShapeDtypeStruct((image_count, width), BF16),
        [SMEM] + [VMEM] * 8,
        (place, packed, by4, by2, by1, by5, by3, near_pairs, far_pairs),
        [pltpu.VMEM((N_BLOCKS, *block), BF16)],
    )
    portion = portion.reshape(2 * X_SIZE, rows, width)
    image_grad = jnp.sum(lax.all_to_all(portion, "section", 0, 0).astype(F32), axis=0)
    return (gated_out[None], image_grad[None])


def solution(mesh):
    in_specs = (
        P("section", "dp", "tensor"),
        P("section", "dp", "tensor"),
        P("section", "tensor", "dp"),
        P("section", "tensor", "dp"),
        P("dp", "section", "tensor"),
        P("dp", None),
        P("section"),
        P("section", "dp", "tensor"),
    )
    out_specs = (P("section", "dp", "tensor"), P("dp", "section", "tensor"))
    return jax.shard_map(local, mesh=mesh, in_specs=in_specs, out_specs=out_specs, check_vma=False)
```

```python
import jax
import jax.numpy as jnp
from jax import lax
from jax.experimental import pallas as pl
from jax.experimental.pallas import tpu as pltpu
from jax.sharding import PartitionSpec as P

HEAD_SIZE = 128
X_SIZE = 4
Y_SIZE = 4
N_BLOCKS = 8
DEPTH = 3
BF16 = jnp.bfloat16
F32 = jnp.float32
VMEM = pl.BlockSpec(memory_space=pltpu.VMEM)
SMEM = pl.BlockSpec(memory_space=pltpu.SMEM)
BY_ROWS = (((0,), (0,)), ((), ()))
BY_COLUMNS = (((1,), (1,)), ((), ()))


def z_swap(a):
    return lax.ppermute(a, "section", [(s, (s + X_SIZE) % (2 * X_SIZE)) for s in range(2 * X_SIZE)])


def x_exchange(a):
    groups = [[z * X_SIZE + x for x in range(X_SIZE)] for z in range(2)]
    return lax.all_to_all(a, "section", 0, 0, axis_index_groups=groups)


def t_swap(a, k):
    return lax.ppermute(a, "tensor", [(t, t ^ k) for t in range(8)])


def y_shift(a, k):
    pairs = [(y * 2 + c, ((y + k) % Y_SIZE) * 2 + c) for y in range(Y_SIZE) for c in range(2)]
    return lax.ppermute(a, "dp", pairs)


def y_gather(a):
    groups = [[2 * y + c for y in range(Y_SIZE)] for c in range(2)]
    copies = jnp.broadcast_to(a[None], (Y_SIZE, *a.shape))
    return lax.all_to_all(copies, "dp", 0, 0, axis_index_groups=groups)


def core_swap(a):
    return lax.ppermute(a, "dp", [(d, d ^ 1) for d in range(2 * Y_SIZE)])


def dot(a, b, dims=None):
    if dims is None:
        return jnp.dot(a, b, preferred_element_type=F32)
    return lax.dot_general(a, b, dims, preferred_element_type=F32)


def call(kernel, outs, in_specs, args, scratch=(), limit=10 << 20, cost=None):
    return pl.pallas_call(
        kernel,
        out_shape=outs,
        in_specs=in_specs,
        out_specs=jax.tree.map(lambda _: VMEM, outs),
        scratch_shapes=scratch,
        cost_estimate=cost,
        compiler_params=pltpu.CompilerParams(vmem_limit_bytes=limit),
    )(*args)


def spread_kernel(own, other, out):
    for x in range(X_SIZE):
        out[x, 0] = own[...]
        out[x, 1] = other[...]


def pair_kernel(head_ref, half_ref, images, near, far, out):
    rows = jnp.concatenate(
        [images[x, half_ref[0] ^ z] for z in range(2) for x in range(X_SIZE)], axis=0
    )
    for slot in range(N_BLOCKS):
        weights = (near, far)[slot % 2][slot // 2]
        out[head_ref[slot]] = dot(rows, weights).astype(BF16)


def query_kernel(dp_ref, features, *refs):
    blocks, (out, rows, columns, sems) = refs[:10], refs[10:]
    cut = columns.shape[1] // 2
    copies = []
    for slot in range(N_BLOCKS):
        group = [pltpu.make_async_copy(features.at[dp_ref[slot]], rows.at[slot], sems.at[0, slot])]
        if slot // 2 == 2:
            for part in range(2):
                group.append(
                    pltpu.make_async_copy(
                        blocks[4 + 2 * part + slot % 2],
                        columns.at[slot, pl.ds(part * cut, cut)],
                        sems.at[1 + part, slot],
                    )
                )
        else:
            at = slot if slot < 4 else slot + 2
            group.append(pltpu.make_async_copy(blocks[at], columns.at[slot], sems.at[1, slot]))
        copies.append(group)
    for group in copies[:DEPTH]:
        for copy in group:
            copy.start()
    total = None
    for slot, group in enumerate(copies):
        for copy in group:
            copy.wait()
        if slot + DEPTH < N_BLOCKS:
            for copy in copies[slot + DEPTH]:
                copy.start()
        part = dot(rows[slot], columns[slot])
        total = part if total is None else total + part
    out[...] = total.astype(BF16)


def attention_kernel(query, arrived, bias_ref, cotangent, gate, gated, packed):
    pairs = jnp.sum(arrived[...].astype(F32), axis=0).astype(BF16)
    keys, values = pairs[:, :HEAD_SIZE], pairs[:, HEAD_SIZE:]
    scaling = HEAD_SIZE ** (-0.5)
    scale_factor = jnp.tanh(gate[...])
    bias = bias_ref[...]
    key_gradient = jnp.zeros((keys.shape[0], HEAD_SIZE), F32)
    value_gradient = key_gradient
    for g in range(query.shape[1] // HEAD_SIZE):
        cols = slice(g * HEAD_SIZE, (g + 1) * HEAD_SIZE)
        q = query[:, cols]
        scores = dot(q, keys, BY_COLUMNS) * scaling + bias
        exponent = jnp.exp(scores - jnp.max(scores, axis=-1, keepdims=True))
        attn_weights = exponent / jnp.sum(exponent, axis=-1, keepdims=True)
        weights_low = attn_weights.astype(BF16)
        gated[:, cols] = (scale_factor * dot(weights_low, values)).astype(BF16)
        attended_gradient = (scale_factor * cotangent[:, cols].astype(F32)).astype(BF16)
        value_gradient += dot(weights_low, attended_gradient, BY_ROWS)
        grad_weights = dot(attended_gradient, values, BY_COLUMNS)
        inner = jnp.sum(attn_weights * grad_weights, axis=-1, keepdims=True)
        grad_low = (attn_weights * (grad_weights - inner)).astype(BF16)
        key_gradient += dot(grad_low, q, BY_ROWS)
    packed[0] = jnp.concatenate(
        [(key_gradient * scaling).astype(BF16), value_gradient.astype(BF16)], axis=1
    )


def image_kernel(place_ref, half_ref, own, by4, by2, by1, by5, by3, near, far, out, buffer):
    for at, part in ((0, own), (1, by4), (2, by2), (4, by1), (5, by5), (6, by3)):
        buffer[at : at + part.shape[0]] = part[...]
    total = None
    for slot in range(N_BLOCKS):
        weights = (near, far)[slot % 2][slot // 2]
        part = dot(buffer[place_ref[slot]], weights, BY_COLUMNS)
        total = part if total is None else total + part
    rows = out.shape[2]
    for z in range(2):
        for x in range(X_SIZE):
            at = (z * X_SIZE + x) * rows
            out[x, z ^ half_ref[0]] = total[at : at + rows].astype(BF16)


def section_kernel(arrived, keep, send):
    total = jnp.sum(arrived[...].astype(F32), axis=0)
    keep[...] = total[0]
    send[...] = total[1].astype(BF16)


def local(
    hidden,
    w_query,
    key_weight_stack,
    value_weight_stack,
    image_tokens,
    score_bias,
    gate_logit,
    cotangent,
):
    tok_rows = hidden.shape[1]
    columns = w_query.shape[2]
    dp = lax.axis_index("dp")
    half = lax.axis_index("section")[None] >> 2
    slots = jnp.arange(N_BLOCKS, dtype=jnp.int32)
    dp_order = ((((dp >> 1) - (slots >> 1)) & (Y_SIZE - 1)) << 1) | ((dp ^ slots) & 1)
    head_order = slots ^ (dp & 1)
    apart = lax.axis_index("tensor") ^ head_order
    place = ((apart & 1) << 2) | (apart & 2) | (apart >> 2)

    features = lax.all_gather(hidden[0], "tensor", axis=0)

    own = image_tokens[0]
    rows, width = own.shape
    pair = jnp.concatenate([key_weight_stack[0], value_weight_stack[0]], axis=1)
    near_pairs, other = lax.optimization_barrier((y_gather(pair), z_swap(own)))

    copies = call(
        spread_kernel,
        jax.ShapeDtypeStruct((X_SIZE, 2, rows, width), BF16),
        [VMEM] * 2,
        (own, other),
    )
    images = x_exchange(copies)
    far_pairs = core_swap(near_pairs)
    image_count = 2 * X_SIZE * rows
    block = (image_count, 2 * HEAD_SIZE)
    portions = call(
        pair_kernel,
        jax.ShapeDtypeStruct((N_BLOCKS, *block), BF16),
        [SMEM] * 2 + [VMEM] * 3,
        (head_order, half, images, near_pairs, far_pairs),
    )
    arrived = lax.all_to_all(portions, "tensor", 0, 0)

    w, _ = lax.optimization_barrier((w_query[0], near_pairs))
    cut = w.shape[0] // 2
    before, behind = y_shift(w, 1), y_shift(w, -1)
    across = (y_shift(before[:cut], 1), y_shift(behind[cut:], -1))
    query_weights = [v for b in (w, before, *across, behind) for v in (b, core_swap(b))]

    tokens, columns = hidden.shape[1], w_query.shape[2]
    query = call(
        query_kernel,
        jax.ShapeDtypeStruct((tokens, columns), BF16),
        [SMEM] + [pl.BlockSpec(memory_space=pl.ANY)] * 11,
        (dp_order, features, *query_weights),
        [
            pltpu.VMEM(features.shape, BF16),
            pltpu.VMEM((N_BLOCKS, *w.shape), BF16),
            pltpu.SemaphoreType.DMA((3, N_BLOCKS)),
        ],
        limit=60 << 20,
        cost=pl.CostEstimate(
            flops=2 * tokens * columns * N_BLOCKS * w.shape[0],
            bytes_accessed=2 * N_BLOCKS * (w.size + hidden.size),
            transcendentals=0,
        ),
    )
    gated_out, packed = call(
        attention_kernel,
        (jax.ShapeDtypeStruct((tokens, columns), BF16), jax.ShapeDtypeStruct((1, *block), BF16)),
        [VMEM] * 5,
        (query, arrived, score_bias, cotangent[0], gate_logit.reshape(1, 1)),
    )

    by4, by1 = lax.optimization_barrier((t_swap(packed, 4), t_swap(packed, 1)))
    both = jnp.concatenate([packed, by4])
    by2, by5 = lax.optimization_barrier((t_swap(both, 2), t_swap(by4, 1)))
    by3 = t_swap(by2, 1)
    portion = call(
        image_kernel,
        jax.ShapeDtypeStruct((X_SIZE, 2, rows, width), BF16),
        [SMEM] * 2 + [VMEM] * 8,
        (place, half, packed, by4, by2, by1, by5, by3, near_pairs, far_pairs),
        [pltpu.VMEM((N_BLOCKS, *block), BF16)],
    )
    keep, send = call(
        section_kernel,
        (jax.ShapeDtypeStruct((rows, width), F32), jax.ShapeDtypeStruct((rows, width), BF16)),
        [VMEM],
        (x_exchange(portion),),
    )
    image_grad = keep + z_swap(send).astype(F32)
    return (gated_out[None], image_grad[None])


def solution(mesh):
    in_specs = (
        P("section", "dp", "tensor"),
        P("section", "dp", "tensor"),
        P("section", "tensor", "dp"),
        P("section", "tensor", "dp"),
        P("dp", "section", "tensor"),
        P("dp", None),
        P("section"),
        P("section", "dp", "tensor"),
    )
    out_specs = (P("section", "dp", "tensor"), P("dp", "section", "tensor"))
    return jax.shard_map(local, mesh=mesh, in_specs=in_specs, out_specs=out_specs, check_vma=False)
```

```python
import jax
import jax.numpy as jnp
from jax import lax
from jax.experimental import pallas as pl
from jax.experimental.pallas import tpu as pltpu
from jax.sharding import PartitionSpec as P

HEAD_SIZE = 128
X_SIZE = 4
Y_SIZE = 4
N_BLOCKS = 8
LATE = (3, 5)
BF16 = jnp.bfloat16
F32 = jnp.float32
VMEM = pl.BlockSpec(memory_space=pltpu.VMEM)
SMEM = pl.BlockSpec(memory_space=pltpu.SMEM)
BY_ROWS = (((0,), (0,)), ((), ()))
BY_COLUMNS = (((1,), (1,)), ((), ()))


def z_swap(a):
    return lax.ppermute(a, "section", [(s, (s + X_SIZE) % (2 * X_SIZE)) for s in range(2 * X_SIZE)])


def x_exchange(a):
    groups = [[z * X_SIZE + x for x in range(X_SIZE)] for z in range(2)]
    return lax.all_to_all(a, "section", 0, 0, axis_index_groups=groups)


def t_swap(a, k):
    return lax.ppermute(a, "tensor", [(t, t ^ k) for t in range(8)])


def y_shift(a, k):
    pairs = [(y * 2 + c, ((y + k) % Y_SIZE) * 2 + c) for y in range(Y_SIZE) for c in range(2)]
    return lax.ppermute(a, "dp", pairs)


def y_gather(a):
    groups = [[2 * y + c for y in range(Y_SIZE)] for c in range(2)]
    copies = jnp.broadcast_to(a[None], (Y_SIZE, *a.shape))
    return lax.all_to_all(copies, "dp", 0, 0, axis_index_groups=groups)


def core_swap(a):
    return lax.ppermute(a, "dp", [(d, d ^ 1) for d in range(2 * Y_SIZE)])


def dot(a, b, dims=None):
    if dims is None:
        return jnp.dot(a, b, preferred_element_type=F32)
    return lax.dot_general(a, b, dims, preferred_element_type=F32)


def call(kernel, outs, in_specs, args, scratch=(), limit=10 << 20, cost=None):
    return pl.pallas_call(
        kernel,
        out_shape=outs,
        in_specs=in_specs,
        out_specs=jax.tree.map(lambda _: VMEM, outs),
        scratch_shapes=scratch,
        cost_estimate=cost,
        compiler_params=pltpu.CompilerParams(vmem_limit_bytes=limit),
    )(*args)


def spread_kernel(own, other, out):
    for x in range(X_SIZE):
        out[x, 0] = own[...]
        out[x, 1] = other[...]


def pair_kernel(head_ref, half_ref, images, near, far, out):
    rows = jnp.concatenate(
        [images[x, half_ref[0] ^ z] for z in range(2) for x in range(X_SIZE)], axis=0
    )
    for slot in range(N_BLOCKS):
        weights = (near, far)[slot % 2][slot // 2]
        out[head_ref[slot]] = dot(rows, weights).astype(BF16)


def query_kernel(dp_ref, features, *refs):
    blocks, (out, rows, columns, sems) = refs[:7], refs[7:]
    cut = columns.shape[1] // 2
    blocks = iter(blocks)
    copies = []
    for slot in range(N_BLOCKS):
        if slot in LATE:
            continue
        group = [pltpu.make_async_copy(features.at[dp_ref[slot]], rows.at[slot], sems.at[0, slot])]
        copies.append((slot, group))
        if slot // 2 != 2:
            group.append(pltpu.make_async_copy(next(blocks), columns.at[slot], sems.at[1, slot]))
            continue
        for part in range(2):
            at = pl.ds(part * cut, cut)
            sem = sems.at[1 + part, slot]
            group.append(pltpu.make_async_copy(next(blocks), columns.at[slot, at], sem))
    for _, group in copies:
        for copy in group:
            copy.start()
    total = None
    for slot, group in copies:
        for copy in group:
            copy.wait()
        part = dot(rows[slot], columns[slot])
        total = part if total is None else total + part
    out[...] = total


def attention_kernel(
    partial, rows, late, upper, lower, arrived, bias_ref, cotangent, gate, gated, packed
):
    cut = upper.shape[0]
    query = partial[...] + dot(rows[0], late[...])
    query = query + dot(rows[1, :, :cut], upper[...]) + dot(rows[1, :, cut:], lower[...])
    query = query.astype(BF16)
    pairs = jnp.sum(arrived[...].astype(F32), axis=0).astype(BF16)
    keys, values = pairs[:, :HEAD_SIZE], pairs[:, HEAD_SIZE:]
    scaling = HEAD_SIZE ** (-0.5)
    scale_factor = jnp.tanh(gate[...])
    bias = bias_ref[...]
    key_gradient = jnp.zeros((keys.shape[0], HEAD_SIZE), F32)
    value_gradient = key_gradient
    for g in range(query.shape[1] // HEAD_SIZE):
        cols = slice(g * HEAD_SIZE, (g + 1) * HEAD_SIZE)
        q = query[:, cols]
        scores = dot(q, keys, BY_COLUMNS) * scaling + bias
        exponent = jnp.exp(scores - jnp.max(scores, axis=-1, keepdims=True))
        attn_weights = exponent / jnp.sum(exponent, axis=-1, keepdims=True)
        weights_low = attn_weights.astype(BF16)
        gated[:, cols] = (scale_factor * dot(weights_low, values)).astype(BF16)
        attended_gradient = (scale_factor * cotangent[:, cols].astype(F32)).astype(BF16)
        value_gradient += dot(weights_low, attended_gradient, BY_ROWS)
        grad_weights = dot(attended_gradient, values, BY_COLUMNS)
        inner = jnp.sum(attn_weights * grad_weights, axis=-1, keepdims=True)
        grad_low = (attn_weights * (grad_weights - inner)).astype(BF16)
        key_gradient += dot(grad_low, q, BY_ROWS)
    packed[0] = jnp.concatenate(
        [(key_gradient * scaling).astype(BF16), value_gradient.astype(BF16)], axis=1
    )


def image_kernel(place_ref, half_ref, own, by4, by2, by1, by5, by3, near, far, out, buffer):
    for at, part in ((0, own), (1, by4), (2, by2), (4, by1), (5, by5), (6, by3)):
        buffer[at : at + part.shape[0]] = part[...]
    total = None
    for slot in range(N_BLOCKS):
        weights = (near, far)[slot % 2][slot // 2]
        part = dot(buffer[place_ref[slot]], weights, BY_COLUMNS)
        total = part if total is None else total + part
    rows = out.shape[2]
    for z in range(2):
        for x in range(X_SIZE):
            at = (z * X_SIZE + x) * rows
            out[x, z ^ half_ref[0]] = total[at : at + rows].astype(BF16)


def section_kernel(arrived, keep, send):
    total = jnp.sum(arrived[...].astype(F32), axis=0)
    keep[...] = total[0]
    send[...] = total[1].astype(BF16)


def local(
    hidden,
    w_query,
    key_weight_stack,
    value_weight_stack,
    image_tokens,
    score_bias,
    gate_logit,
    cotangent,
):
    tok_rows = hidden.shape[1]
    columns = w_query.shape[2]
    dp = lax.axis_index("dp")
    half = lax.axis_index("section")[None] >> 2
    slots = jnp.arange(N_BLOCKS, dtype=jnp.int32)
    dp_order = ((((dp >> 1) - (slots >> 1)) & (Y_SIZE - 1)) << 1) | ((dp ^ slots) & 1)
    head_order = slots ^ (dp & 1)
    apart = lax.axis_index("tensor") ^ head_order
    place = ((apart & 1) << 2) | (apart & 2) | (apart >> 2)

    features = lax.all_gather(hidden[0], "tensor", axis=0)

    own = image_tokens[0]
    rows, width = own.shape
    pair = jnp.concatenate([key_weight_stack[0], value_weight_stack[0]], axis=1)
    near_pairs, other = lax.optimization_barrier((y_gather(pair), z_swap(own)))

    copies = call(
        spread_kernel,
        jax.ShapeDtypeStruct((X_SIZE, 2, rows, width), BF16),
        [VMEM] * 2,
        (own, other),
    )
    images = x_exchange(copies)
    far_pairs = core_swap(near_pairs)
    image_count = 2 * X_SIZE * rows
    block = (image_count, 2 * HEAD_SIZE)
    portions = call(
        pair_kernel,
        jax.ShapeDtypeStruct((N_BLOCKS, *block), BF16),
        [SMEM] * 2 + [VMEM] * 3,
        (head_order, half, images, near_pairs, far_pairs),
    )
    arrived = lax.all_to_all(portions, "tensor", 0, 0)

    w, _ = lax.optimization_barrier((w_query[0], near_pairs))
    cut = w.shape[0] // 2
    before, behind = y_shift(w, 1), y_shift(w, -1)
    across = (y_shift(before[:cut], 1), y_shift(behind[cut:], -1))
    edges = (w, core_swap(w), behind, core_swap(behind))
    features, across, before = lax.optimization_barrier((features, across, before))
    late = [core_swap(v) for v in (before, *across)]
    tokens, columns = hidden.shape[1], w_query.shape[2]
    partial = call(
        query_kernel,
        jax.ShapeDtypeStruct((tokens, columns), F32),
        [SMEM] + [pl.BlockSpec(memory_space=pl.ANY)] * 8,
        (dp_order, features, *edges[:2], before, *across, *edges[2:]),
        [
            pltpu.VMEM(features.shape, BF16),
            pltpu.VMEM((N_BLOCKS, *w.shape), BF16),
            pltpu.SemaphoreType.DMA((3, N_BLOCKS)),
        ],
        limit=60 << 20,
        cost=pl.CostEstimate(
            flops=2 * tokens * columns * (N_BLOCKS - 2) * w.shape[0],
            bytes_accessed=2 * N_BLOCKS * (w.size + hidden.size),
            transcendentals=0,
        ),
    )
    late_rows = jnp.stack(
        [lax.dynamic_index_in_dim(features, dp_order[slot], 0, keepdims=False) for slot in LATE]
    )
    gated_out, packed = call(
        attention_kernel,
        (jax.ShapeDtypeStruct((tokens, columns), BF16), jax.ShapeDtypeStruct((1, *block), BF16)),
        [VMEM] * 9,
        (
            partial,
            late_rows,
            *late,
            arrived,
            score_bias,
            cotangent[0],
            gate_logit.reshape(1, 1),
        ),
    )

    by4, by1 = lax.optimization_barrier((t_swap(packed, 4), t_swap(packed, 1)))
    both = jnp.concatenate([packed, by4])
    by2, by5 = lax.optimization_barrier((t_swap(both, 2), t_swap(by4, 1)))
    by3 = t_swap(by2, 1)
    portion = call(
        image_kernel,
        jax.ShapeDtypeStruct((X_SIZE, 2, rows, width), BF16),
        [SMEM] * 2 + [VMEM] * 8,
        (place, half, packed, by4, by2, by1, by5, by3, near_pairs, far_pairs),
        [pltpu.VMEM((N_BLOCKS, *block), BF16)],
    )
    keep, send = call(
        section_kernel,
        (jax.ShapeDtypeStruct((rows, width), F32), jax.ShapeDtypeStruct((rows, width), BF16)),
        [VMEM],
        (x_exchange(portion),),
    )
    image_grad = keep + z_swap(send).astype(F32)
    return (gated_out[None], image_grad[None])


def solution(mesh):
    in_specs = (
        P("section", "dp", "tensor"),
        P("section", "dp", "tensor"),
        P("section", "tensor", "dp"),
        P("section", "tensor", "dp"),
        P("dp", "section", "tensor"),
        P("dp", None),
        P("section"),
        P("section", "dp", "tensor"),
    )
    out_specs = (P("section", "dp", "tensor"), P("dp", "section", "tensor"))
    return jax.shard_map(local, mesh=mesh, in_specs=in_specs, out_specs=out_specs, check_vma=False)
```

```python
import jax
import jax.numpy as jnp
from jax import lax
from jax.experimental import pallas as pl
from jax.experimental.pallas import tpu as pltpu
from jax.sharding import PartitionSpec as P

HEAD_SIZE = 128
X_SIZE = 4
Y_SIZE = 4
N_BLOCKS = 8
DEPTH = 3
BF16 = jnp.bfloat16
F32 = jnp.float32
VMEM = pl.BlockSpec(memory_space=pltpu.VMEM)
SMEM = pl.BlockSpec(memory_space=pltpu.SMEM)
BY_ROWS = (((0,), (0,)), ((), ()))
BY_COLUMNS = (((1,), (1,)), ((), ()))


def z_swap(a):
    return lax.ppermute(a, "section", [(s, (s + X_SIZE) % (2 * X_SIZE)) for s in range(2 * X_SIZE)])


def x_exchange(a):
    groups = [[z * X_SIZE + x for x in range(X_SIZE)] for z in range(2)]
    return lax.all_to_all(a, "section", 0, 0, axis_index_groups=groups)


def t_swap(a, k):
    return lax.ppermute(a, "tensor", [(t, t ^ k) for t in range(8)])


def y_shift(a, k):
    pairs = [(y * 2 + c, ((y + k) % Y_SIZE) * 2 + c) for y in range(Y_SIZE) for c in range(2)]
    return lax.ppermute(a, "dp", pairs)


def y_gather(a):
    groups = [[2 * y + c for y in range(Y_SIZE)] for c in range(2)]
    copies = jnp.broadcast_to(a[None], (Y_SIZE, *a.shape))
    return lax.all_to_all(copies, "dp", 0, 0, axis_index_groups=groups)


def core_swap(a):
    return lax.ppermute(a, "dp", [(d, d ^ 1) for d in range(2 * Y_SIZE)])


def dot(a, b, dims=None):
    if dims is None:
        return jnp.dot(a, b, preferred_element_type=F32)
    return lax.dot_general(a, b, dims, preferred_element_type=F32)


def call(kernel, outs, in_specs, args, scratch=(), limit=10 << 20, cost=None):
    return pl.pallas_call(
        kernel,
        out_shape=outs,
        in_specs=in_specs,
        out_specs=jax.tree.map(lambda _: VMEM, outs),
        scratch_shapes=scratch,
        cost_estimate=cost,
        compiler_params=pltpu.CompilerParams(vmem_limit_bytes=limit),
    )(*args)


def spread_kernel(own, other, out):
    for x in range(X_SIZE):
        out[x, 0] = own[...]
        out[x, 1] = other[...]


def pair_kernel(head_ref, half_ref, images, near, far, out):
    rows = jnp.concatenate(
        [images[x, half_ref[0] ^ z] for z in range(2) for x in range(X_SIZE)], axis=0
    )
    for slot in range(N_BLOCKS):
        weights = (near, far)[slot % 2][slot // 2]
        out[head_ref[slot]] = dot(rows, weights).astype(BF16)


def query_kernel(dp_ref, features, *refs):
    blocks, (out, rows, columns, sems) = refs[:10], refs[10:]
    cut = columns.shape[1] // 2
    copies = []
    for slot in range(N_BLOCKS):
        group = [pltpu.make_async_copy(features.at[dp_ref[slot]], rows.at[slot], sems.at[0, slot])]
        if slot // 2 == 2:
            for part in range(2):
                group.append(
                    pltpu.make_async_copy(
                        blocks[4 + 2 * part + slot % 2],
                        columns.at[slot, pl.ds(part * cut, cut)],
                        sems.at[1 + part, slot],
                    )
                )
        else:
            at = slot if slot < 4 else slot + 2
            group.append(pltpu.make_async_copy(blocks[at], columns.at[slot], sems.at[1, slot]))
        copies.append(group)
    for group in copies[:DEPTH]:
        for copy in group:
            copy.start()
    total = None
    for slot, group in enumerate(copies):
        for copy in group:
            copy.wait()
        if slot + DEPTH < N_BLOCKS:
            for copy in copies[slot + DEPTH]:
                copy.start()
        part = dot(rows[slot], columns[slot])
        total = part if total is None else total + part
    out[...] = total.astype(BF16)


def attention_kernel(query, arrived, bias_ref, cotangent, gate, gated, packed):
    pairs = jnp.sum(arrived[...].astype(F32), axis=0).astype(BF16)
    keys, values = pairs[:, :HEAD_SIZE], pairs[:, HEAD_SIZE:]
    scaling = HEAD_SIZE ** (-0.5)
    scale_factor = jnp.tanh(gate[...])
    bias = bias_ref[...]
    key_gradient = jnp.zeros((keys.shape[0], HEAD_SIZE), F32)
    value_gradient = key_gradient
    for g in range(query.shape[1] // HEAD_SIZE):
        cols = slice(g * HEAD_SIZE, (g + 1) * HEAD_SIZE)
        q = query[:, cols]
        scores = dot(q, keys, BY_COLUMNS) * scaling + bias
        exponent = jnp.exp(scores - jnp.max(scores, axis=-1, keepdims=True))
        attn_weights = exponent / jnp.sum(exponent, axis=-1, keepdims=True)
        weights_low = attn_weights.astype(BF16)
        gated[:, cols] = (scale_factor * dot(weights_low, values)).astype(BF16)
        attended_gradient = (scale_factor * cotangent[:, cols].astype(F32)).astype(BF16)
        value_gradient += dot(weights_low, attended_gradient, BY_ROWS)
        grad_weights = dot(attended_gradient, values, BY_COLUMNS)
        inner = jnp.sum(attn_weights * grad_weights, axis=-1, keepdims=True)
        grad_low = (attn_weights * (grad_weights - inner)).astype(BF16)
        key_gradient += dot(grad_low, q, BY_ROWS)
    packed[0] = jnp.concatenate(
        [(key_gradient * scaling).astype(BF16), value_gradient.astype(BF16)], axis=1
    )


def head_products(y_ref, parts, even, odd):
    total = None
    for part, distance in parts:
        weights = (even, odd)[distance & 1][y_ref[distance]]
        product = dot(part, weights, BY_COLUMNS)
        total = product if total is None else total + product
    return total


def early_image_kernel(y_ref, flip_ref, own, by4, by2, by1, by5, near, far, out):
    parts = [(own[0], 0), (by4[0], 4), (by2[0], 2), (by2[1], 6), (by1[0], 1), (by5[0], 5)]

    @pl.when(flip_ref[0] == 0)
    def _():
        out[...] = head_products(y_ref, parts, near, far)

    @pl.when(flip_ref[0] != 0)
    def _():
        out[...] = head_products(y_ref, parts, far, near)


def late_image_kernel(y_ref, flip_ref, half_ref, early, by3, near, far, out, total):
    parts = [(by3[0], 3), (by3[1], 7)]

    @pl.when(flip_ref[0] == 0)
    def _():
        total[...] = early[...] + head_products(y_ref, parts, near, far)

    @pl.when(flip_ref[0] != 0)
    def _():
        total[...] = early[...] + head_products(y_ref, parts, far, near)

    rows = out.shape[2]
    for z in range(2):
        for x in range(X_SIZE):
            at = (z * X_SIZE + x) * rows
            out[x, z ^ half_ref[0]] = total[at : at + rows].astype(BF16)


def section_kernel(arrived, keep, send):
    total = jnp.sum(arrived[...].astype(F32), axis=0)
    keep[...] = total[0]
    send[...] = total[1].astype(BF16)


def local(
    hidden,
    w_query,
    key_weight_stack,
    value_weight_stack,
    image_tokens,
    score_bias,
    gate_logit,
    cotangent,
):
    tok_rows = hidden.shape[1]
    columns = w_query.shape[2]
    dp = lax.axis_index("dp")
    half = lax.axis_index("section")[None] >> 2
    slots = jnp.arange(N_BLOCKS, dtype=jnp.int32)
    dp_order = ((((dp >> 1) - (slots >> 1)) & (Y_SIZE - 1)) << 1) | ((dp ^ slots) & 1)
    head_order = slots ^ (dp & 1)
    tensor = lax.axis_index("tensor")
    head_y = (tensor ^ slots) >> 1
    flip = ((tensor ^ dp) & 1)[None]

    features = lax.all_gather(hidden[0], "tensor", axis=0)

    own = image_tokens[0]
    rows, width = own.shape
    pair = jnp.concatenate([key_weight_stack[0], value_weight_stack[0]], axis=1)
    near_pairs, other = lax.optimization_barrier((y_gather(pair), z_swap(own)))

    copies = call(
        spread_kernel,
        jax.ShapeDtypeStruct((X_SIZE, 2, rows, width), BF16),
        [VMEM] * 2,
        (own, other),
    )
    images = x_exchange(copies)
    far_pairs = core_swap(near_pairs)
    image_count = 2 * X_SIZE * rows
    block = (image_count, 2 * HEAD_SIZE)
    portions = call(
        pair_kernel,
        jax.ShapeDtypeStruct((N_BLOCKS, *block), BF16),
        [SMEM] * 2 + [VMEM] * 3,
        (head_order, half, images, near_pairs, far_pairs),
    )
    arrived = lax.all_to_all(portions, "tensor", 0, 0)

    w, _ = lax.optimization_barrier((w_query[0], near_pairs))
    cut = w.shape[0] // 2
    before, behind = y_shift(w, 1), y_shift(w, -1)
    across = (y_shift(before[:cut], 1), y_shift(behind[cut:], -1))
    query_weights = [v for b in (w, before, *across, behind) for v in (b, core_swap(b))]

    tokens, columns = hidden.shape[1], w_query.shape[2]
    query = call(
        query_kernel,
        jax.ShapeDtypeStruct((tokens, columns), BF16),
        [SMEM] + [pl.BlockSpec(memory_space=pl.ANY)] * 11,
        (dp_order, features, *query_weights),
        [
            pltpu.VMEM(features.shape, BF16),
            pltpu.VMEM((N_BLOCKS, *w.shape), BF16),
            pltpu.SemaphoreType.DMA((3, N_BLOCKS)),
        ],
        limit=60 << 20,
        cost=pl.CostEstimate(
            flops=2 * tokens * columns * N_BLOCKS * w.shape[0],
            bytes_accessed=2 * N_BLOCKS * (w.size + hidden.size),
            transcendentals=0,
        ),
    )
    gated_out, packed = call(
        attention_kernel,
        (jax.ShapeDtypeStruct((tokens, columns), BF16), jax.ShapeDtypeStruct((1, *block), BF16)),
        [VMEM] * 5,
        (query, arrived, score_bias, cotangent[0], gate_logit.reshape(1, 1)),
    )

    by4, by1 = lax.optimization_barrier((t_swap(packed, 4), t_swap(packed, 1)))
    both = jnp.concatenate([packed, by4])
    by2, by5 = lax.optimization_barrier((t_swap(both, 2), t_swap(by4, 1)))
    by3 = t_swap(by2, 1)
    early = call(
        early_image_kernel,
        jax.ShapeDtypeStruct((image_count, width), F32),
        [SMEM] * 2 + [VMEM] * 7,
        (head_y, flip, packed, by4, by2, by1, by5, near_pairs, far_pairs),
        cost=pl.CostEstimate(
            flops=12 * packed.size * width,
            bytes_accessed=12 * packed.size + 4 * near_pairs.size + 4 * image_count * width,
            transcendentals=0,
        ),
    )
    portion = call(
        late_image_kernel,
        jax.ShapeDtypeStruct((X_SIZE, 2, rows, width), BF16),
        [SMEM] * 3 + [VMEM] * 4,
        (head_y, flip, half, early, by3, near_pairs, far_pairs),
        [pltpu.VMEM((image_count, width), F32)],
    )
    keep, send = call(
        section_kernel,
        (jax.ShapeDtypeStruct((rows, width), F32), jax.ShapeDtypeStruct((rows, width), BF16)),
        [VMEM],
        (x_exchange(portion),),
    )
    image_grad = keep + z_swap(send).astype(F32)
    return (gated_out[None], image_grad[None])


def solution(mesh):
    in_specs = (
        P("section", "dp", "tensor"),
        P("section", "dp", "tensor"),
        P("section", "tensor", "dp"),
        P("section", "tensor", "dp"),
        P("dp", "section", "tensor"),
        P("dp", None),
        P("section"),
        P("section", "dp", "tensor"),
    )
    out_specs = (P("section", "dp", "tensor"), P("dp", "section", "tensor"))
    return jax.shard_map(local, mesh=mesh, in_specs=in_specs, out_specs=out_specs, check_vma=False)
```

```python
import jax
import jax.numpy as jnp
from jax import lax
from jax.experimental import pallas as pl
from jax.experimental.pallas import tpu as pltpu
from jax.sharding import PartitionSpec as P

HEAD_SIZE = 128
X_SIZE = 4
Y_SIZE = 4
N_BLOCKS = 8
DEPTH = 3
BF16 = jnp.bfloat16
F32 = jnp.float32
VMEM = pl.BlockSpec(memory_space=pltpu.VMEM)
SMEM = pl.BlockSpec(memory_space=pltpu.SMEM)
BY_ROWS = (((0,), (0,)), ((), ()))
BY_COLUMNS = (((1,), (1,)), ((), ()))


def z_swap(a):
    return lax.ppermute(a, "section", [(s, (s + X_SIZE) % (2 * X_SIZE)) for s in range(2 * X_SIZE)])


def x_exchange(a):
    groups = [[z * X_SIZE + x for x in range(X_SIZE)] for z in range(2)]
    return lax.all_to_all(a, "section", 0, 0, axis_index_groups=groups)


def t_swap(a, k):
    return lax.ppermute(a, "tensor", [(t, t ^ k) for t in range(8)])


def y_shift(a, k):
    pairs = [(y * 2 + c, ((y + k) % Y_SIZE) * 2 + c) for y in range(Y_SIZE) for c in range(2)]
    return lax.ppermute(a, "dp", pairs)


def y_gather(a):
    groups = [[2 * y + c for y in range(Y_SIZE)] for c in range(2)]
    copies = jnp.broadcast_to(a[None], (Y_SIZE, *a.shape))
    return lax.all_to_all(copies, "dp", 0, 0, axis_index_groups=groups)


def core_swap(a):
    return lax.ppermute(a, "dp", [(d, d ^ 1) for d in range(2 * Y_SIZE)])


def dot(a, b, dims=None):
    if dims is None:
        return jnp.dot(a, b, preferred_element_type=F32)
    return lax.dot_general(a, b, dims, preferred_element_type=F32)


def call(kernel, outs, in_specs, args, scratch=(), limit=10 << 20, cost=None):
    return pl.pallas_call(
        kernel,
        out_shape=outs,
        in_specs=in_specs,
        out_specs=jax.tree.map(lambda _: VMEM, outs),
        scratch_shapes=scratch,
        cost_estimate=cost,
        compiler_params=pltpu.CompilerParams(vmem_limit_bytes=limit),
    )(*args)


def spread_kernel(own, other, out):
    for x in range(X_SIZE):
        out[x, 0] = own[...]
        out[x, 1] = other[...]


def pair_kernel(head_ref, half_ref, images, near, far, out):
    rows = jnp.concatenate(
        [images[x, half_ref[0] ^ z] for z in range(2) for x in range(X_SIZE)], axis=0
    )
    for slot in range(N_BLOCKS):
        weights = (near, far)[slot % 2][slot // 2]
        out[head_ref[slot]] = dot(rows, weights).astype(BF16)


def query_kernel(dp_ref, features, *refs):
    blocks, (out, rows, columns, sems) = refs[:10], refs[10:]
    cut = columns.shape[1] // 2
    copies = []
    for slot in range(N_BLOCKS):
        group = [pltpu.make_async_copy(features.at[dp_ref[slot]], rows.at[slot], sems.at[0, slot])]
        if slot // 2 == 2:
            for part in range(2):
                group.append(
                    pltpu.make_async_copy(
                        blocks[4 + 2 * part + slot % 2],
                        columns.at[slot, pl.ds(part * cut, cut)],
                        sems.at[1 + part, slot],
                    )
                )
        else:
            at = slot if slot < 4 else slot + 2
            group.append(pltpu.make_async_copy(blocks[at], columns.at[slot], sems.at[1, slot]))
        copies.append(group)
    for group in copies[:DEPTH]:
        for copy in group:
            copy.start()
    total = None
    for slot, group in enumerate(copies):
        for copy in group:
            copy.wait()
        if slot + DEPTH < N_BLOCKS:
            for copy in copies[slot + DEPTH]:
                copy.start()
        part = dot(rows[slot], columns[slot])
        total = part if total is None else total + part
    out[...] = total.astype(BF16)


def attention_kernel(query, arrived, bias_ref, cotangent, gate, gated, packed):
    pairs = jnp.sum(arrived[...].astype(F32), axis=0).astype(BF16)
    keys, values = pairs[:, :HEAD_SIZE], pairs[:, HEAD_SIZE:]
    scaling = HEAD_SIZE ** (-0.5)
    scale_factor = jnp.tanh(gate[...])
    bias = bias_ref[...]
    key_gradient = jnp.zeros((keys.shape[0], HEAD_SIZE), F32)
    value_gradient = key_gradient
    for g in range(query.shape[1] // HEAD_SIZE):
        cols = slice(g * HEAD_SIZE, (g + 1) * HEAD_SIZE)
        q = query[:, cols]
        scores = dot(q, keys, BY_COLUMNS) * scaling + bias
        exponent = jnp.exp(scores - jnp.max(scores, axis=-1, keepdims=True))
        attn_weights = exponent / jnp.sum(exponent, axis=-1, keepdims=True)
        weights_low = attn_weights.astype(BF16)
        gated[:, cols] = (scale_factor * dot(weights_low, values)).astype(BF16)
        attended_gradient = (scale_factor * cotangent[:, cols].astype(F32)).astype(BF16)
        value_gradient += dot(weights_low, attended_gradient, BY_ROWS)
        grad_weights = dot(attended_gradient, values, BY_COLUMNS)
        inner = jnp.sum(attn_weights * grad_weights, axis=-1, keepdims=True)
        grad_low = (attn_weights * (grad_weights - inner)).astype(BF16)
        key_gradient += dot(grad_low, q, BY_ROWS)
    packed[0] = jnp.concatenate(
        [(key_gradient * scaling).astype(BF16), value_gradient.astype(BF16)], axis=1
    )


def head_products(y_ref, parts, even, odd):
    total = None
    for part, distance in parts:
        weights = (even, odd)[distance & 1][y_ref[distance]]
        product = dot(part, weights, BY_COLUMNS)
        total = product if total is None else total + product
    return total


def early_image_kernel(y_ref, flip_ref, own, by4, by2, by1, by5, near, far, out):
    parts = [(own[0], 0), (by4[0], 4), (by2[0], 2), (by2[1], 6), (by1[0], 1), (by5[0], 5)]

    @pl.when(flip_ref[0] == 0)
    def _():
        out[...] = head_products(y_ref, parts, near, far)

    @pl.when(flip_ref[0] != 0)
    def _():
        out[...] = head_products(y_ref, parts, far, near)


def late_image_kernel(y_ref, flip_ref, half_ref, early, by3, near, far, out, total):
    parts = [(by3[0], 3), (by3[1], 7)]

    @pl.when(flip_ref[0] == 0)
    def _():
        total[...] = early[...] + head_products(y_ref, parts, near, far)

    @pl.when(flip_ref[0] != 0)
    def _():
        total[...] = early[...] + head_products(y_ref, parts, far, near)

    rows = out.shape[2]
    for z in range(2):
        for x in range(X_SIZE):
            at = (z * X_SIZE + x) * rows
            out[x, z ^ half_ref[0]] = total[at : at + rows].astype(BF16)


def section_kernel(arrived, keep, send):
    total = jnp.sum(arrived[...].astype(F32), axis=0)
    keep[...] = total[0]
    send[...] = total[1].astype(BF16)


def local(
    hidden,
    w_query,
    key_weight_stack,
    value_weight_stack,
    image_tokens,
    score_bias,
    gate_logit,
    cotangent,
):
    tok_rows = hidden.shape[1]
    columns = w_query.shape[2]
    dp = lax.axis_index("dp")
    half = lax.axis_index("section")[None] >> 2
    slots = jnp.arange(N_BLOCKS, dtype=jnp.int32)
    dp_order = ((((dp >> 1) - (slots >> 1)) & (Y_SIZE - 1)) << 1) | ((dp ^ slots) & 1)
    head_order = slots ^ (dp & 1)
    tensor = lax.axis_index("tensor")
    head_y = (tensor ^ slots) >> 1
    flip = ((tensor ^ dp) & 1)[None]

    features = lax.all_gather(hidden[0], "tensor", axis=0)

    own = image_tokens[0]
    rows, width = own.shape
    pair = jnp.concatenate([key_weight_stack[0], value_weight_stack[0]], axis=1)
    near_pairs, other = lax.optimization_barrier((y_gather(pair), z_swap(own)))

    copies = call(
        spread_kernel,
        jax.ShapeDtypeStruct((X_SIZE, 2, rows, width), BF16),
        [VMEM] * 2,
        (own, other),
    )
    images = x_exchange(copies)
    far_pairs = core_swap(near_pairs)
    image_count = 2 * X_SIZE * rows
    block = (image_count, 2 * HEAD_SIZE)
    portions = call(
        pair_kernel,
        jax.ShapeDtypeStruct((N_BLOCKS, *block), BF16),
        [SMEM] * 2 + [VMEM] * 3,
        (head_order, half, images, near_pairs, far_pairs),
    )
    arrived = lax.all_to_all(portions, "tensor", 0, 0)

    w, _ = lax.optimization_barrier((w_query[0], near_pairs))
    cut = w.shape[0] // 2
    before, behind = y_shift(w, 1), y_shift(w, -1)
    across = (y_shift(before[:cut], 1), y_shift(behind[cut:], -1))
    features, across, before = lax.optimization_barrier((features, across, before))
    query_weights = [v for b in (w, before, *across, behind) for v in (b, core_swap(b))]

    tokens, columns = hidden.shape[1], w_query.shape[2]
    query = call(
        query_kernel,
        jax.ShapeDtypeStruct((tokens, columns), BF16),
        [SMEM] + [pl.BlockSpec(memory_space=pl.ANY)] * 11,
        (dp_order, features, *query_weights),
        [
            pltpu.VMEM(features.shape, BF16),
            pltpu.VMEM((N_BLOCKS, *w.shape), BF16),
            pltpu.SemaphoreType.DMA((3, N_BLOCKS)),
        ],
        limit=60 << 20,
        cost=pl.CostEstimate(
            flops=2 * tokens * columns * N_BLOCKS * w.shape[0],
            bytes_accessed=2 * N_BLOCKS * (w.size + hidden.size),
            transcendentals=0,
        ),
    )
    gated_out, packed = call(
        attention_kernel,
        (jax.ShapeDtypeStruct((tokens, columns), BF16), jax.ShapeDtypeStruct((1, *block), BF16)),
        [VMEM] * 5,
        (query, arrived, score_bias, cotangent[0], gate_logit.reshape(1, 1)),
    )

    by4, by1 = lax.optimization_barrier((t_swap(packed, 4), t_swap(packed, 1)))
    both = jnp.concatenate([packed, by4])
    by2, by5 = lax.optimization_barrier((t_swap(both, 2), t_swap(by4, 1)))
    by3 = t_swap(by2, 1)
    early = call(
        early_image_kernel,
        jax.ShapeDtypeStruct((image_count, width), F32),
        [SMEM] * 2 + [VMEM] * 7,
        (head_y, flip, packed, by4, by2, by1, by5, near_pairs, far_pairs),
        cost=pl.CostEstimate(
            flops=12 * packed.size * width,
            bytes_accessed=12 * packed.size + 4 * near_pairs.size + 4 * image_count * width,
            transcendentals=0,
        ),
    )
    portion = call(
        late_image_kernel,
        jax.ShapeDtypeStruct((X_SIZE, 2, rows, width), BF16),
        [SMEM] * 3 + [VMEM] * 4,
        (head_y, flip, half, early, by3, near_pairs, far_pairs),
        [pltpu.VMEM((image_count, width), F32)],
    )
    keep, send = call(
        section_kernel,
        (jax.ShapeDtypeStruct((rows, width), F32), jax.ShapeDtypeStruct((rows, width), BF16)),
        [VMEM],
        (x_exchange(portion),),
    )
    image_grad = keep + z_swap(send).astype(F32)
    return (gated_out[None], image_grad[None])


def solution(mesh):
    in_specs = (
        P("section", "dp", "tensor"),
        P("section", "dp", "tensor"),
        P("section", "tensor", "dp"),
        P("section", "tensor", "dp"),
        P("dp", "section", "tensor"),
        P("dp", None),
        P("section"),
        P("section", "dp", "tensor"),
    )
    out_specs = (P("section", "dp", "tensor"), P("dp", "section", "tensor"))
    return jax.shard_map(local, mesh=mesh, in_specs=in_specs, out_specs=out_specs, check_vma=False)
```

```python
import jax
import jax.numpy as jnp
from jax import lax
from jax.experimental import pallas as pl
from jax.experimental.pallas import tpu as pltpu
from jax.sharding import PartitionSpec as P

HEAD_SIZE = 128
X_SIZE = 4
Y_SIZE = 4
N_BLOCKS = 8
DEPTH = 3
BF16 = jnp.bfloat16
F32 = jnp.float32
VMEM = pl.BlockSpec(memory_space=pltpu.VMEM)
SMEM = pl.BlockSpec(memory_space=pltpu.SMEM)
BY_ROWS = (((0,), (0,)), ((), ()))
BY_COLUMNS = (((1,), (1,)), ((), ()))


def z_swap(a):
    return lax.ppermute(a, "section", [(s, (s + X_SIZE) % (2 * X_SIZE)) for s in range(2 * X_SIZE)])


def x_exchange(a):
    groups = [[z * X_SIZE + x for x in range(X_SIZE)] for z in range(2)]
    return lax.all_to_all(a, "section", 0, 0, axis_index_groups=groups)


def t_swap(a, k):
    return lax.ppermute(a, "tensor", [(t, t ^ k) for t in range(8)])


def y_shift(a, k):
    pairs = [(y * 2 + c, ((y + k) % Y_SIZE) * 2 + c) for y in range(Y_SIZE) for c in range(2)]
    return lax.ppermute(a, "dp", pairs)


def y_gather(a):
    groups = [[2 * y + c for y in range(Y_SIZE)] for c in range(2)]
    copies = jnp.broadcast_to(a[None], (Y_SIZE, *a.shape))
    return lax.all_to_all(copies, "dp", 0, 0, axis_index_groups=groups)


def core_swap(a):
    return lax.ppermute(a, "dp", [(d, d ^ 1) for d in range(2 * Y_SIZE)])


def dot(a, b, dims=None):
    if dims is None:
        return jnp.dot(a, b, preferred_element_type=F32)
    return lax.dot_general(a, b, dims, preferred_element_type=F32)


def call(kernel, outs, in_specs, args, scratch=(), limit=10 << 20, cost=None):
    return pl.pallas_call(
        kernel,
        out_shape=outs,
        in_specs=in_specs,
        out_specs=jax.tree.map(lambda _: VMEM, outs),
        scratch_shapes=scratch,
        cost_estimate=cost,
        compiler_params=pltpu.CompilerParams(vmem_limit_bytes=limit),
    )(*args)


def spread_kernel(own, other, out):
    for x in range(X_SIZE):
        out[x, 0] = own[...]
        out[x, 1] = other[...]


def pair_kernel(head_ref, half_ref, images, near, far, out):
    rows = jnp.concatenate(
        [images[x, half_ref[0] ^ z] for z in range(2) for x in range(X_SIZE)], axis=0
    )
    for slot in range(N_BLOCKS):
        weights = (near, far)[slot % 2][slot // 2]
        out[head_ref[slot]] = dot(rows, weights).astype(BF16)


def query_kernel(dp_ref, features, *refs):
    blocks, (out, rows, columns, sems) = refs[:N_BLOCKS], refs[N_BLOCKS:]
    copies = []
    for slot in range(N_BLOCKS):
        copies.append(
            (
                pltpu.make_async_copy(features.at[dp_ref[slot]], rows.at[slot], sems.at[0, slot]),
                pltpu.make_async_copy(blocks[slot], columns.at[slot], sems.at[1, slot]),
            )
        )
    for group in copies[:DEPTH]:
        for copy in group:
            copy.start()
    total = None
    for slot, group in enumerate(copies):
        for copy in group:
            copy.wait()
        if slot + DEPTH < N_BLOCKS:
            for copy in copies[slot + DEPTH]:
                copy.start()
        part = dot(rows[slot], columns[slot])
        total = part if total is None else total + part
    out[...] = total.astype(BF16)


def attention_kernel(query, arrived, bias_ref, cotangent, gate, gated, packed):
    pairs = jnp.sum(arrived[...].astype(F32), axis=0).astype(BF16)
    keys, values = pairs[:, :HEAD_SIZE], pairs[:, HEAD_SIZE:]
    scaling = HEAD_SIZE ** (-0.5)
    scale_factor = jnp.tanh(gate[...])
    bias = bias_ref[...]
    key_gradient = jnp.zeros((keys.shape[0], HEAD_SIZE), F32)
    value_gradient = key_gradient
    for g in range(query.shape[1] // HEAD_SIZE):
        cols = slice(g * HEAD_SIZE, (g + 1) * HEAD_SIZE)
        q = query[:, cols]
        scores = dot(q, keys, BY_COLUMNS) * scaling + bias
        exponent = jnp.exp(scores - jnp.max(scores, axis=-1, keepdims=True))
        attn_weights = exponent / jnp.sum(exponent, axis=-1, keepdims=True)
        weights_low = attn_weights.astype(BF16)
        gated[:, cols] = (scale_factor * dot(weights_low, values)).astype(BF16)
        attended_gradient = (scale_factor * cotangent[:, cols].astype(F32)).astype(BF16)
        value_gradient += dot(weights_low, attended_gradient, BY_ROWS)
        grad_weights = dot(attended_gradient, values, BY_COLUMNS)
        inner = jnp.sum(attn_weights * grad_weights, axis=-1, keepdims=True)
        grad_low = (attn_weights * (grad_weights - inner)).astype(BF16)
        key_gradient += dot(grad_low, q, BY_ROWS)
    packed[0] = jnp.concatenate(
        [(key_gradient * scaling).astype(BF16), value_gradient.astype(BF16)], axis=1
    )


def head_products(y_ref, parts, even, odd):
    total = None
    for part, distance in parts:
        weights = (even, odd)[distance & 1][y_ref[distance]]
        product = dot(part, weights, BY_COLUMNS)
        total = product if total is None else total + product
    return total


def early_image_kernel(y_ref, flip_ref, own, by4, by2, by1, by5, near, far, out):
    parts = [(own[0], 0), (by4[0], 4), (by2[0], 2), (by2[1], 6), (by1[0], 1), (by5[0], 5)]

    @pl.when(flip_ref[0] == 0)
    def _():
        out[...] = head_products(y_ref, parts, near, far)

    @pl.when(flip_ref[0] != 0)
    def _():
        out[...] = head_products(y_ref, parts, far, near)


def late_image_kernel(y_ref, flip_ref, half_ref, early, by3, near, far, out, total):
    parts = [(by3[0], 3), (by3[1], 7)]

    @pl.when(flip_ref[0] == 0)
    def _():
        total[...] = early[...] + head_products(y_ref, parts, near, far)

    @pl.when(flip_ref[0] != 0)
    def _():
        total[...] = early[...] + head_products(y_ref, parts, far, near)

    rows = out.shape[2]
    for z in range(2):
        for x in range(X_SIZE):
            at = (z * X_SIZE + x) * rows
            out[x, z ^ half_ref[0]] = total[at : at + rows].astype(BF16)


def section_kernel(arrived, keep, send):
    total = jnp.sum(arrived[...].astype(F32), axis=0)
    keep[...] = total[0]
    send[...] = total[1].astype(BF16)


def local(
    hidden,
    w_query,
    key_weight_stack,
    value_weight_stack,
    image_tokens,
    score_bias,
    gate_logit,
    cotangent,
):
    tok_rows = hidden.shape[1]
    columns = w_query.shape[2]
    dp = lax.axis_index("dp")
    half = lax.axis_index("section")[None] >> 2
    slots = jnp.arange(N_BLOCKS, dtype=jnp.int32)
    dp_order = ((((dp >> 1) - (slots >> 1)) & (Y_SIZE - 1)) << 1) | ((dp ^ slots) & 1)
    head_order = slots ^ (dp & 1)
    tensor = lax.axis_index("tensor")
    head_y = (tensor ^ slots) >> 1
    flip = ((tensor ^ dp) & 1)[None]

    features = lax.all_gather(hidden[0], "tensor", axis=0)

    own = image_tokens[0]
    rows, width = own.shape
    pair = jnp.concatenate([key_weight_stack[0], value_weight_stack[0]], axis=1)
    near_pairs, other = lax.optimization_barrier((y_gather(pair), z_swap(own)))

    copies = call(
        spread_kernel,
        jax.ShapeDtypeStruct((X_SIZE, 2, rows, width), BF16),
        [VMEM] * 2,
        (own, other),
    )
    images = x_exchange(copies)
    far_pairs = core_swap(near_pairs)
    image_count = 2 * X_SIZE * rows
    block = (image_count, 2 * HEAD_SIZE)
    portions = call(
        pair_kernel,
        jax.ShapeDtypeStruct((N_BLOCKS, *block), BF16),
        [SMEM] * 2 + [VMEM] * 3,
        (head_order, half, images, near_pairs, far_pairs),
    )
    arrived = lax.all_to_all(portions, "tensor", 0, 0)

    w, _ = lax.optimization_barrier((w_query[0], near_pairs))
    before, opposite, behind = y_shift(w, 1), y_shift(w, 2), y_shift(w, -1)
    features, opposite, before = lax.optimization_barrier((features, opposite, before))
    query_weights = [v for b in (w, before, opposite, behind) for v in (b, core_swap(b))]

    tokens, columns = hidden.shape[1], w_query.shape[2]
    query = call(
        query_kernel,
        jax.ShapeDtypeStruct((tokens, columns), BF16),
        [SMEM] + [pl.BlockSpec(memory_space=pl.ANY)] * 9,
        (dp_order, features, *query_weights),
        [
            pltpu.VMEM(features.shape, BF16),
            pltpu.VMEM((N_BLOCKS, *w.shape), BF16),
            pltpu.SemaphoreType.DMA((2, N_BLOCKS)),
        ],
        limit=60 << 20,
        cost=pl.CostEstimate(
            flops=2 * tokens * columns * N_BLOCKS * w.shape[0],
            bytes_accessed=2 * N_BLOCKS * (w.size + hidden.size),
            transcendentals=0,
        ),
    )
    gated_out, packed = call(
        attention_kernel,
        (jax.ShapeDtypeStruct((tokens, columns), BF16), jax.ShapeDtypeStruct((1, *block), BF16)),
        [VMEM] * 5,
        (query, arrived, score_bias, cotangent[0], gate_logit.reshape(1, 1)),
    )

    by1, by4 = lax.optimization_barrier((t_swap(packed, 1), t_swap(packed, 4)))
    both = jnp.concatenate([packed, by4])
    by2, by5 = lax.optimization_barrier((t_swap(both, 2), t_swap(by4, 1)))
    by3 = t_swap(by2, 1)
    early = call(
        early_image_kernel,
        jax.ShapeDtypeStruct((image_count, width), F32),
        [SMEM] * 2 + [VMEM] * 7,
        (head_y, flip, packed, by4, by2, by1, by5, near_pairs, far_pairs),
        cost=pl.CostEstimate(
            flops=12 * packed.size * width,
            bytes_accessed=12 * packed.size + 4 * near_pairs.size + 4 * image_count * width,
            transcendentals=0,
        ),
    )
    portion = call(
        late_image_kernel,
        jax.ShapeDtypeStruct((X_SIZE, 2, rows, width), BF16),
        [SMEM] * 3 + [VMEM] * 4,
        (head_y, flip, half, early, by3, near_pairs, far_pairs),
        [pltpu.VMEM((image_count, width), F32)],
    )
    keep, send = call(
        section_kernel,
        (jax.ShapeDtypeStruct((rows, width), F32), jax.ShapeDtypeStruct((rows, width), BF16)),
        [VMEM],
        (x_exchange(portion),),
    )
    image_grad = keep + z_swap(send).astype(F32)
    return (gated_out[None], image_grad[None])


def solution(mesh):
    in_specs = (
        P("section", "dp", "tensor"),
        P("section", "dp", "tensor"),
        P("section", "tensor", "dp"),
        P("section", "tensor", "dp"),
        P("dp", "section", "tensor"),
        P("dp", None),
        P("section"),
        P("section", "dp", "tensor"),
    )
    out_specs = (P("section", "dp", "tensor"), P("dp", "section", "tensor"))
    return jax.shard_map(local, mesh=mesh, in_specs=in_specs, out_specs=out_specs, check_vma=False)
```

```python
import jax
import jax.numpy as jnp
from jax import lax
from jax.experimental import pallas as pl
from jax.experimental.pallas import tpu as pltpu
from jax.sharding import PartitionSpec as P

HEAD_SIZE = 128
X_SIZE = 4
Y_SIZE = 4
N_BLOCKS = 8
DEPTH = 3
BF16 = jnp.bfloat16
F32 = jnp.float32
VMEM = pl.BlockSpec(memory_space=pltpu.VMEM)
SMEM = pl.BlockSpec(memory_space=pltpu.SMEM)
BY_ROWS = (((0,), (0,)), ((), ()))
BY_COLUMNS = (((1,), (1,)), ((), ()))


def z_swap(a):
    return lax.ppermute(a, "section", [(s, (s + X_SIZE) % (2 * X_SIZE)) for s in range(2 * X_SIZE)])


def x_exchange(a):
    groups = [[z * X_SIZE + x for x in range(X_SIZE)] for z in range(2)]
    return lax.all_to_all(a, "section", 0, 0, axis_index_groups=groups)


def t_swap(a, k):
    return lax.ppermute(a, "tensor", [(t, t ^ k) for t in range(8)])


def y_shift(a, k):
    pairs = [(y * 2 + c, ((y + k) % Y_SIZE) * 2 + c) for y in range(Y_SIZE) for c in range(2)]
    return lax.ppermute(a, "dp", pairs)


def y_gather(a):
    groups = [[2 * y + c for y in range(Y_SIZE)] for c in range(2)]
    copies = jnp.broadcast_to(a[None], (Y_SIZE, *a.shape))
    return lax.all_to_all(copies, "dp", 0, 0, axis_index_groups=groups)


def core_swap(a):
    return lax.ppermute(a, "dp", [(d, d ^ 1) for d in range(2 * Y_SIZE)])


def dot(a, b, dims=None):
    if dims is None:
        return jnp.dot(a, b, preferred_element_type=F32)
    return lax.dot_general(a, b, dims, preferred_element_type=F32)


def call(kernel, outs, in_specs, args, scratch=(), limit=10 << 20, cost=None):
    return pl.pallas_call(
        kernel,
        out_shape=outs,
        in_specs=in_specs,
        out_specs=jax.tree.map(lambda _: VMEM, outs),
        scratch_shapes=scratch,
        cost_estimate=cost,
        compiler_params=pltpu.CompilerParams(vmem_limit_bytes=limit),
    )(*args)


def spread_kernel(own, other, out):
    for x in range(X_SIZE):
        out[x, 0] = own[...]
        out[x, 1] = other[...]


def pair_kernel(head_ref, half_ref, images, near, far, out):
    rows = jnp.concatenate(
        [images[x, half_ref[0] ^ z] for z in range(2) for x in range(X_SIZE)], axis=0
    )
    for slot in range(N_BLOCKS):
        weights = (near, far)[slot % 2][slot // 2]
        out[head_ref[slot]] = dot(rows, weights).astype(BF16)


def attention_kernel(dp_ref, features, *refs):
    blocks, refs = refs[:N_BLOCKS], refs[N_BLOCKS:]
    arrived, bias_ref, cotangent, gate, gated, packed, rows, columns, sems = refs
    copies = []
    for slot in range(N_BLOCKS):
        copies.append(
            (
                pltpu.make_async_copy(features.at[dp_ref[slot]], rows.at[slot], sems.at[0, slot]),
                pltpu.make_async_copy(blocks[slot], columns.at[slot], sems.at[1, slot]),
            )
        )
    for group in copies[:DEPTH]:
        for copy in group:
            copy.start()
    total = None
    for slot, group in enumerate(copies):
        for copy in group:
            copy.wait()
        if slot + DEPTH < N_BLOCKS:
            for copy in copies[slot + DEPTH]:
                copy.start()
        part = dot(rows[slot], columns[slot])
        total = part if total is None else total + part
    query = total.astype(BF16)

    pairs = jnp.sum(arrived[...].astype(F32), axis=0).astype(BF16)
    keys, values = pairs[:, :HEAD_SIZE], pairs[:, HEAD_SIZE:]
    scaling = HEAD_SIZE ** (-0.5)
    scale_factor = jnp.tanh(gate[...])
    bias = bias_ref[...]
    key_gradient = jnp.zeros((keys.shape[0], HEAD_SIZE), F32)
    value_gradient = key_gradient
    for g in range(query.shape[1] // HEAD_SIZE):
        cols = slice(g * HEAD_SIZE, (g + 1) * HEAD_SIZE)
        q = query[:, cols]
        scores = dot(q, keys, BY_COLUMNS) * scaling + bias
        exponent = jnp.exp(scores - jnp.max(scores, axis=-1, keepdims=True))
        attn_weights = exponent / jnp.sum(exponent, axis=-1, keepdims=True)
        weights_low = attn_weights.astype(BF16)
        gated[:, cols] = (scale_factor * dot(weights_low, values)).astype(BF16)
        attended_gradient = (scale_factor * cotangent[:, cols].astype(F32)).astype(BF16)
        value_gradient += dot(weights_low, attended_gradient, BY_ROWS)
        grad_weights = dot(attended_gradient, values, BY_COLUMNS)
        inner = jnp.sum(attn_weights * grad_weights, axis=-1, keepdims=True)
        grad_low = (attn_weights * (grad_weights - inner)).astype(BF16)
        key_gradient += dot(grad_low, q, BY_ROWS)
    packed[0] = jnp.concatenate(
        [(key_gradient * scaling).astype(BF16), value_gradient.astype(BF16)], axis=1
    )


def head_products(y_ref, parts, even, odd):
    total = None
    for part, distance in parts:
        weights = (even, odd)[distance & 1][y_ref[distance]]
        product = dot(part, weights, BY_COLUMNS)
        total = product if total is None else total + product
    return total


def early_image_kernel(y_ref, flip_ref, own, by4, by2, by1, by5, near, far, out):
    parts = [(own[0], 0), (by4[0], 4), (by2[0], 2), (by2[1], 6), (by1[0], 1), (by5[0], 5)]

    @pl.when(flip_ref[0] == 0)
    def _():
        out[...] = head_products(y_ref, parts, near, far)

    @pl.when(flip_ref[0] != 0)
    def _():
        out[...] = head_products(y_ref, parts, far, near)


def late_image_kernel(y_ref, flip_ref, half_ref, early, by3, near, far, out, total):
    parts = [(by3[0], 3), (by3[1], 7)]

    @pl.when(flip_ref[0] == 0)
    def _():
        total[...] = early[...] + head_products(y_ref, parts, near, far)

    @pl.when(flip_ref[0] != 0)
    def _():
        total[...] = early[...] + head_products(y_ref, parts, far, near)

    rows = out.shape[2]
    for z in range(2):
        for x in range(X_SIZE):
            at = (z * X_SIZE + x) * rows
            out[x, z ^ half_ref[0]] = total[at : at + rows].astype(BF16)


def section_kernel(arrived, keep, send):
    total = jnp.sum(arrived[...].astype(F32), axis=0)
    keep[...] = total[0]
    send[...] = total[1].astype(BF16)


def local(
    hidden,
    w_query,
    key_weight_stack,
    value_weight_stack,
    image_tokens,
    score_bias,
    gate_logit,
    cotangent,
):
    tok_rows = hidden.shape[1]
    columns = w_query.shape[2]
    dp = lax.axis_index("dp")
    half = lax.axis_index("section")[None] >> 2
    slots = jnp.arange(N_BLOCKS, dtype=jnp.int32)
    dp_order = ((((dp >> 1) - (slots >> 1)) & (Y_SIZE - 1)) << 1) | ((dp ^ slots) & 1)
    head_order = slots ^ (dp & 1)
    tensor = lax.axis_index("tensor")
    head_y = (tensor ^ slots) >> 1
    flip = ((tensor ^ dp) & 1)[None]

    features = lax.all_gather(hidden[0], "tensor", axis=0)

    own = image_tokens[0]
    rows, width = own.shape
    pair = jnp.concatenate([key_weight_stack[0], value_weight_stack[0]], axis=1)
    near_pairs, other = lax.optimization_barrier((y_gather(pair), z_swap(own)))

    copies = call(
        spread_kernel,
        jax.ShapeDtypeStruct((X_SIZE, 2, rows, width), BF16),
        [VMEM] * 2,
        (own, other),
    )
    images = x_exchange(copies)
    far_pairs = core_swap(near_pairs)
    image_count = 2 * X_SIZE * rows
    block = (image_count, 2 * HEAD_SIZE)
    portions = call(
        pair_kernel,
        jax.ShapeDtypeStruct((N_BLOCKS, *block), BF16),
        [SMEM] * 2 + [VMEM] * 3,
        (head_order, half, images, near_pairs, far_pairs),
    )
    arrived = lax.all_to_all(portions, "tensor", 0, 0)

    w, _ = lax.optimization_barrier((w_query[0], near_pairs))
    before, opposite, behind = y_shift(w, 1), y_shift(w, 2), y_shift(w, -1)
    features, opposite, before = lax.optimization_barrier((features, opposite, before))
    query_weights = [v for b in (w, before, opposite, behind) for v in (b, core_swap(b))]

    tokens, columns = hidden.shape[1], w_query.shape[2]
    gated_out, packed = call(
        attention_kernel,
        (jax.ShapeDtypeStruct((tokens, columns), BF16), jax.ShapeDtypeStruct((1, *block), BF16)),
        [SMEM] + [pl.BlockSpec(memory_space=pl.ANY)] * 9 + [VMEM] * 4,
        (
            dp_order,
            features,
            *query_weights,
            arrived,
            score_bias,
            cotangent[0],
            gate_logit.reshape(1, 1),
        ),
        [
            pltpu.VMEM(features.shape, BF16),
            pltpu.VMEM((N_BLOCKS, *w.shape), BF16),
            pltpu.SemaphoreType.DMA((2, N_BLOCKS)),
        ],
        limit=60 << 20,
        cost=pl.CostEstimate(
            flops=2 * tokens * columns * N_BLOCKS * w.shape[0],
            bytes_accessed=2 * N_BLOCKS * (w.size + hidden.size),
            transcendentals=0,
        ),
    )

    by1, by4 = lax.optimization_barrier((t_swap(packed, 1), t_swap(packed, 4)))
    both = jnp.concatenate([packed, by4])
    by2, by5 = lax.optimization_barrier((t_swap(both, 2), t_swap(by4, 1)))
    by3 = t_swap(by2, 1)
    early = call(
        early_image_kernel,
        jax.ShapeDtypeStruct((image_count, width), F32),
        [SMEM] * 2 + [VMEM] * 7,
        (head_y, flip, packed, by4, by2, by1, by5, near_pairs, far_pairs),
        cost=pl.CostEstimate(
            flops=12 * packed.size * width,
            bytes_accessed=12 * packed.size + 4 * near_pairs.size + 4 * image_count * width,
            transcendentals=0,
        ),
    )
    portion = call(
        late_image_kernel,
        jax.ShapeDtypeStruct((X_SIZE, 2, rows, width), BF16),
        [SMEM] * 3 + [VMEM] * 4,
        (head_y, flip, half, early, by3, near_pairs, far_pairs),
        [pltpu.VMEM((image_count, width), F32)],
    )
    keep, send = call(
        section_kernel,
        (jax.ShapeDtypeStruct((rows, width), F32), jax.ShapeDtypeStruct((rows, width), BF16)),
        [VMEM],
        (x_exchange(portion),),
    )
    image_grad = keep + z_swap(send).astype(F32)
    return (gated_out[None], image_grad[None])


def solution(mesh):
    in_specs = (
        P("section", "dp", "tensor"),
        P("section", "dp", "tensor"),
        P("section", "tensor", "dp"),
        P("section", "tensor", "dp"),
        P("dp", "section", "tensor"),
        P("dp", None),
        P("section"),
        P("section", "dp", "tensor"),
    )
    out_specs = (P("section", "dp", "tensor"), P("dp", "section", "tensor"))
    return jax.shard_map(local, mesh=mesh, in_specs=in_specs, out_specs=out_specs, check_vma=False)
```
